256 devices in a mesh: row: 64 (over x_hi, y, z), col: 4 (over x_lo, core).
Axes of the slice: x: 4 (x_hi: 2, x_lo: 2; x = x_hi * 2 + x_lo), y: 4, z: 8, core: 2. Of those that a mesh axis runs over, the one named last changes fastest.
Arguments:
- weights: bfloat16 [3, 8192, 28672], P(None, 'row', 'col'), may hold values from -6 to 6
- left_outer: bfloat16 [64, 64], replicated, may hold values from -0.75 to 0.75
- left_inner: bfloat16 [128, 128], replicated, may hold values from -0.5 to 0.5
- right_outer: bfloat16 [224, 224], replicated, may hold values from -0.375 to 0.375
- right_inner: bfloat16 [128, 128], replicated, may hold values from -0.5 to 0.5
Outputs:
- rotated: bfloat16 [3, 128, 64, 28672], P(None, 'row', None, 'col')
- scales: float32 [3, 128, 64, 224], P(None, 'row', None, 'col')
The draws below stay inside these ranges and needn't reach their ends.
All inputs are finite; a program needn't handle non-finite values.
Results may differ from the reference program's by a relative error of at most 0.0064.
Values may be sent and summed in bfloat16 or wider, within the bound.
No kernel may reach another device: no remote copies, remote signals or barrier semaphores. Data moves between devices by JAX's collectives and lax.ppermute only.
A program may use at most 128 MiB of HBM per device.

```python
import jax
import jax.numpy as jnp
from jax import lax

D = 8192
FF = 28672
BD = 128
BF = 128
MATS = 3
DA = 64
FA = 224


def shard_levels(stream_key, shape, pieces, least, largest):
    def one(dim, blocks):
        steps = jax.random.uniform(jax.random.fold_in(jax.random.fold_in(stream_key, 6), dim), (blocks,), jnp.float32, least / len(pieces), largest / len(pieces))
        return jnp.repeat(jnp.exp(steps), shape[dim] // blocks).reshape((-1,) + (1,) * (len(shape) - dim - 1))

    loudness = one(*pieces[0])
    for cut in pieces[1:]:
        loudness = loudness * one(*cut)
    return loudness


def centred(stream_key, extent, spread, limit, pieces=(), kind=jnp.bfloat16):
    gain = shard_levels(stream_key, extent, pieces, -0.22, 0.18) if pieces else 1.0
    array = jax.random.normal(stream_key, extent, jnp.float32) * spread * gain
    return jnp.minimum(jnp.maximum(array, -limit), limit).astype(kind)


def setup_inputs(seed: int = 0) -> dict:
    key_of = jax.random.split(jax.random.key(seed), 6)
    return {
        "weights": centred(key_of[0], (MATS, D, FF), 1.0, 6.0, ((1, 64), (2, 4))),
        "left_outer": centred(key_of[1], (DA, DA), DA ** -0.5, 0.75),
        "left_inner": centred(key_of[2], (BD, BD), BD ** -0.5, 0.5),
        "right_outer": centred(key_of[3], (FA, FA), FA ** -0.5, 0.375),
        "right_inner": centred(key_of[4], (BF, BF), BF ** -0.5, 0.5),
    }


def reference(weights, left_outer, left_inner, right_outer, right_inner):
    lo_f = left_outer.astype(jnp.float32)
    li_f = left_inner.astype(jnp.float32)
    ro_f = right_outer.astype(jnp.float32)
    ri_f = right_inner.astype(jnp.float32)

    def local_pass(block):
        first = jnp.einsum("bpk,qk->bpq", block.astype(jnp.float32), ri_f).astype(jnp.bfloat16)
        return jnp.einsum("bk,kpq->bpq", li_f, first.astype(jnp.float32)).astype(jnp.bfloat16)

    def outer_pass(block):
        third = jnp.einsum("ak,kpq->apq", lo_f, block.astype(jnp.float32)).astype(jnp.bfloat16)
        return jnp.einsum("pk,akq->apq", ro_f, third.astype(jnp.float32)).astype(jnp.bfloat16)

    def one_matrix(matrix):
        shaped = matrix.reshape(DA, BD, FA, BF)
        second = lax.map(local_pass, shaped)
        moved = jnp.moveaxis(second, 1, 0)
        mixed = lax.map(outer_pass, moved)
        block_max = jnp.max(jnp.abs(mixed.astype(jnp.float32)), axis=-1) / 1.5
        return mixed.reshape(BD, DA, FF), block_max

    rotated, scales = lax.map(one_matrix, weights)
    return rotated, scales
```

```python
import jax
import jax.numpy as jnp
import numpy as np
from jax import lax
from jax.experimental import pallas as pl
from jax.experimental.pallas import tpu as pltpu
from jax.sharding import Mesh
from jax.sharding import PartitionSpec as P

BF16 = jnp.bfloat16
F32 = jnp.float32
XH, Y, Z, XL, CORE = "xh", "y", "z", "xl", "core"
AXES = (XH, Y, Z, XL, CORE)
SIZES = (2, 4, 8, 2, 2)
WIDTH = 7168
BLOCKS = 56
STRIDE_IN = 232
STRIDE_OUT = 24
VMEM = 40 * 1024 * 1024


def matmul(left, right):
    return jnp.dot(left, right, preferred_element_type=F32)


def inner_kernel(w_ref, li_ref, ri_ref, o_ref):
    ri = ri_ref[...]
    parts = []
    for p in range(w_ref.shape[2] // 128):
        block = w_ref[0, :, p * 128 : (p + 1) * 128]
        parts.append(
            lax.dot_general(
                block, ri, (((1,), (1,)), ((), ())), preferred_element_type=F32
            ).astype(BF16)
        )
    o_ref[...] = matmul(li_ref[...], jnp.concatenate(parts, axis=1)).astype(BF16)


def inner(weights, index, li, ri):
    tile = 896
    return pl.pallas_call(
        inner_kernel,
        grid=(WIDTH // tile,),
        in_specs=[
            pl.BlockSpec((1, 128, tile), lambda i: (index, 0, i)),
            pl.BlockSpec((128, 128), lambda i: (0, 0)),
            pl.BlockSpec((128, 128), lambda i: (0, 0)),
        ],
        out_specs=pl.BlockSpec((128, tile), lambda i: (0, i)),
        out_shape=jax.ShapeDtypeStruct((128, WIDTH), BF16),
        compiler_params=pltpu.CompilerParams(vmem_limit_bytes=VMEM),
        cost_estimate=pl.CostEstimate(
            flops=4 * 128 * 128 * WIDTH, bytes_accessed=4 * 128 * WIDTH, transcendentals=0
        ),
        name="inner",
    )(weights, li, ri)


def outer_kernel(own0, own1, other0, other1, ro_ref, o_ref, gathered, mixed):
    for source, ref in enumerate((own0, own1, other0, other1)):
        for p in range(BLOCKS):
            gathered[pl.ds(source * BLOCKS + p, 16, stride=STRIDE_IN), :] = ref[
                :, p * 128 : (p + 1) * 128
            ].astype(F32)
    ro = ro_ref[...]
    for group in range(4):
        rows = range(group * 4, group * 4 + 4)
        columns = jnp.concatenate(
            [
                gathered[r * STRIDE_IN : r * STRIDE_IN + 4 * BLOCKS, :].astype(BF16)
                for r in rows
            ],
            axis=1,
        )
        result = matmul(ro, columns)
        for at, r in enumerate(rows):
            mixed[pl.ds(r, 2 * BLOCKS, stride=STRIDE_OUT), :] = result[
                :, at * 128 : (at + 1) * 128
            ]
    for p in range(BLOCKS):
        for half in range(2):
            first = p * STRIDE_OUT + half * 8
            second = (BLOCKS + p) * STRIDE_OUT + half * 8
            both = jnp.concatenate(
                [mixed[first : first + 8, :], mixed[second : second + 8, :]], axis=0
            )
            o_ref[half * 16 : half * 16 + 16, p * 128 : (p + 1) * 128] = both.astype(BF16)


def outer_right(own, other, ro):
    spec = lambda half: pl.BlockSpec((16, WIDTH), lambda i: (i + 4 * half, 0))
    return pl.pallas_call(
        outer_kernel,
        grid=(4,),
        in_specs=[
            spec(0),
            spec(1),
            spec(0),
            spec(1),
            pl.BlockSpec((2 * BLOCKS, 4 * BLOCKS), lambda i: (0, 0)),
        ],
        out_specs=pl.BlockSpec((32, WIDTH), lambda i: (i, 0)),
        out_shape=jax.ShapeDtypeStruct((128, WIDTH), BF16),
        scratch_shapes=[
            pltpu.VMEM((16 * STRIDE_IN, 128), F32),
            pltpu.VMEM((2 * BLOCKS * STRIDE_OUT, 128), F32),
        ],
        compiler_params=pltpu.CompilerParams(vmem_limit_bytes=VMEM),
        cost_estimate=pl.CostEstimate(
            flops=8 * 64 * BLOCKS * WIDTH,
            bytes_accessed=10 * 128 * WIDTH,
            transcendentals=0,
        ),
        name="outer_right",
    )(own, own, other, other, ro)


def block_scales(values, first, held):
    lanes = lax.broadcasted_iota(jnp.int32, held.shape, 1)
    for p in range(values.shape[1] // 128):
        block = jnp.abs(values[:, p * 128 : (p + 1) * 128].astype(F32))
        largest = jnp.max(block, axis=1, keepdims=True) / 1.5
        held = jnp.where(lanes == first + p, largest, held)
    return held


def last_kernel(x_ref, lo_ref, *refs):
    o_ref, s_ref, held = refs[-3:]
    step = pl.program_id(0)
    tile = x_ref.shape[1]
    values = matmul(lo_ref[...], x_ref[...]).astype(BF16)
    o_ref[...] = values.reshape(1, 2, 64, tile)
    scales = block_scales(values, step * (tile // 128), held[...])
    held[...] = scales
    s_ref[...] = scales[:, :BLOCKS].reshape(1, 2, 64, BLOCKS)


def last(x, lo, index, rotated, scales):
    tile = 1792
    return pl.pallas_call(
        last_kernel,
        grid=(WIDTH // tile,),
        in_specs=[
            pl.BlockSpec((128, tile), lambda i: (0, i)),
            pl.BlockSpec((128, 128), lambda i: (0, 0)),
            pl.BlockSpec(memory_space=pl.ANY),
            pl.BlockSpec(memory_space=pl.ANY),
        ],
        out_specs=[
            pl.BlockSpec((1, 2, 64, tile), lambda i: (index, 0, 0, i)),
            pl.BlockSpec((1, 2, 64, BLOCKS), lambda i: (index, 0, 0, 0)),
        ],
        out_shape=[
            jax.ShapeDtypeStruct((3, 2, 64, WIDTH), BF16),
            jax.ShapeDtypeStruct((3, 2, 64, BLOCKS), F32),
        ],
        scratch_shapes=[pltpu.VMEM((128, 128), F32)],
        input_output_aliases={2: 0, 3: 1},
        compiler_params=pltpu.CompilerParams(vmem_limit_bytes=VMEM),
        cost_estimate=pl.CostEstimate(
            flops=2 * 128 * 128 * WIDTH, bytes_accessed=4 * 128 * WIDTH, transcendentals=0
        ),
        name="last",
    )(x, lo, rotated, scales)


def place_kernel(flip_ref, x_ref, o_ref, s_ref, held):
    step = pl.program_id(1)
    tile = x_ref.shape[2]
    values = x_ref[0]
    o_ref[...] = values.reshape(1, 1, 64, tile)
    scales = block_scales(values, step * (tile // 128), held[...])
    held[...] = scales
    s_ref[...] = scales[:, :BLOCKS].reshape(1, 1, 64, BLOCKS)


def place(x, flip):
    tile = 1792
    return pl.pallas_call(
        place_kernel,
        grid_spec=pltpu.PrefetchScalarGridSpec(
            num_scalar_prefetch=1,
            grid=(2, WIDTH // tile),
            in_specs=[
                pl.BlockSpec((1, 64, tile), lambda h, i, flip: (h ^ flip[0], 0, i))
            ],
            out_specs=[
                pl.BlockSpec((1, 1, 64, tile), lambda h, i, flip: (0, h, 0, i)),
                pl.BlockSpec((1, 1, 64, BLOCKS), lambda h, i, flip: (0, h, 0, 0)),
            ],
            scratch_shapes=[pltpu.VMEM((64, 128), F32)],
        ),
        out_shape=[
            jax.ShapeDtypeStruct((3, 2, 64, WIDTH), BF16),
            jax.ShapeDtypeStruct((3, 2, 64, BLOCKS), F32),
        ],
        compiler_params=pltpu.CompilerParams(vmem_limit_bytes=VMEM),
        cost_estimate=pl.CostEstimate(
            flops=128 * WIDTH, bytes_accessed=4 * 128 * WIDTH, transcendentals=0
        ),
        name="place",
    )(flip, x)


def swap(x, axis):
    return lax.ppermute(x, axis, [(0, 1), (1, 0)])


def exchange_z(x):
    slabs = [x[16 * d : 16 * (d + 1)] for d in range(8)]
    moved = {0: slabs[0]}
    for d in (4, 3, 5, 2, 6, 1, 7):
        moved[d] = lax.ppermute(slabs[d], Z, [(i, (i + d) % 8) for i in range(8)])
    return jnp.concatenate([moved[d] for d in range(8)], axis=0)


def exchange_xy(x):
    received = lax.all_to_all(
        x.reshape(16, 8, WIDTH), (XH, Y, XL), split_axis=0, concat_axis=0, tiled=True
    )
    return received.reshape(128, WIDTH)


def one_hot(order, size):
    return (order[:, None] == jnp.arange(size, dtype=jnp.int32)[None, :]).astype(BF16)


def moved_rows(order):
    return jnp.asarray(np.eye(128)[order.reshape(-1)], BF16)


def reorder(matrix, x):
    return matmul(matrix, x).astype(BF16)


def local(weights, left_outer, left_inner, right_outer, right_inner):
    z, xl, core = lax.axis_index(Z), lax.axis_index(XL), lax.axis_index(CORE)
    index = jnp.arange(128, dtype=jnp.int32)

    def inner_rows(xy, dz, parity):
        return matmul(
            one_hot(xy * 16 + (z + dz) % 8 * 2 + parity, 128), left_inner
        ).astype(BF16)

    li0 = inner_rows(index // 2 % 8, index // 16, index % 2)
    li1 = inner_rows(index % 8, index // 8 % 8, (index // 64) ^ xl)
    li2 = inner_rows(index // 8 % 8, index % 8, (index // 64) ^ xl)

    column = jnp.arange(64, dtype=jnp.int32)
    back = one_hot(column // 8 * 8 + (z - column % 8) % 8, 64)
    lo = lax.dot_general(
        left_outer, back, (((1,), (1,)), ((), ())), preferred_element_type=F32
    ).astype(BF16)
    lo = lo.reshape(1, 64, 8, 1, 8) * jnp.eye(2, dtype=BF16).reshape(2, 1, 1, 2, 1)
    lo01 = lo.reshape(128, 128)
    lo2 = lo.transpose(0, 1, 4, 2, 3).reshape(128, 128)

    ro = right_outer.reshape(2, 2, BLOCKS, 2, 2, BLOCKS)
    ro = jnp.where(core == 0, ro[:, 0], ro[:, 1, :, :, ::-1])
    ro = ro.transpose(0, 1, 3, 2, 4)
    ro0 = jnp.where(xl == 0, ro, ro[::-1]).reshape(2 * BLOCKS, 4 * BLOCKS)
    ro12 = jnp.where(xl == 0, ro, ro[:, :, :, ::-1]).reshape(2 * BLOCKS, 4 * BLOCKS)

    rows = np.arange(128)
    to_xy0 = moved_rows(rows.reshape(8, 16).T)
    to_xy1 = moved_rows(rows.reshape(8, 2, 8).transpose(2, 1, 0))
    to_z2 = moved_rows(rows.reshape(16, 8).T)

    def hidden_first(matrix, li):
        sent = inner(weights, matrix, li, right_inner)
        own = jnp.concatenate([sent[:64], swap(sent[64:], XL)], axis=0)
        return outer_right(own, swap(own, CORE), ro12)

    first0 = exchange_z(inner(weights, 0, li0, right_inner))
    mixed2 = hidden_first(2, li2)
    mixed1 = hidden_first(1, li1)
    received2 = exchange_z(reorder(to_z2, exchange_xy(mixed2)))

    third0 = reorder(lo01, exchange_xy(reorder(to_xy0, first0)))
    mixed0 = outer_right(third0, swap(third0, CORE), ro0).reshape(8, 2, 8, WIDTH)
    halves = jnp.stack(
        [
            mixed0[:, 0].reshape(64, WIDTH),
            swap(mixed0[:, 1].reshape(64, WIDTH), XL),
        ]
    )
    rotated, scales = place(halves, jnp.full((1,), xl, jnp.int32))

    received1 = exchange_xy(reorder(to_xy1, exchange_z(mixed1)))
    rotated, scales = last(received1, lo01, 1, rotated, scales)
    rotated, scales = last(received2, lo2, 2, rotated, scales)
    return rotated, scales


def solution(mesh):
    fine = Mesh(np.asarray(mesh.devices).reshape(SIZES), AXES)
    row, col = (XH, Y, Z), (XL, CORE)
    return jax.shard_map(
        local,
        mesh=fine,
        in_specs=(P(None, row, col), P(), P(), P(), P()),
        out_specs=(P(None, row, None, col), P(None, row, None, col)),
        check_vma=False,
    )
```

```python
import functools

import jax
import jax.numpy as jnp
import numpy as np
from jax import lax
from jax.experimental import pallas as pl
from jax.experimental.pallas import tpu as pltpu
from jax.sharding import Mesh
from jax.sharding import PartitionSpec as P

BF16 = jnp.bfloat16
F32 = jnp.float32
XH, Y, Z, XL, CORE = "xh", "y", "z", "xl", "core"
AXES = (XH, Y, Z, XL, CORE)
SIZES = (2, 4, 8, 2, 2)
WIDTH = 7168
BLOCKS = 56
VMEM = 24 * 1024 * 1024
INNER_VMEM = 60 * 1024 * 1024
WHOLE = pl.BlockSpec(memory_space=pltpu.VMEM)
ORDER = pl.BlockSpec(memory_space=pl.ANY)


def matmul(left, right):
    return jnp.dot(left, right, preferred_element_type=F32)


def blocks_of(count):
    return jax.ShapeDtypeStruct((count, BLOCKS, 128), BF16)


def cost(flops, passes):
    return pl.CostEstimate(
        flops=flops, bytes_accessed=passes * 128 * WIDTH * 2, transcendentals=0
    )


def inner_kernel(matrix, outs, xl_ref, w_ref, li_ref, ri_ref, *refs):
    o_refs, (held, turned, packed, sems, out_sems) = refs[-5 - outs : -5], refs[-5:]
    tiles = 4
    tile = WIDTH // tiles
    copies = [
        pltpu.make_async_copy(
            w_ref.at[matrix, :, pl.ds(t * tile, tile)], held.at[t], sems.at[t]
        )
        for t in range(tiles)
    ]
    for copy in copies:
        copy.start()
    ri = ri_ref[...]
    zero = jnp.zeros_like(ri)
    pair = jnp.concatenate(
        [
            jnp.concatenate([ri, zero], axis=1),
            jnp.concatenate([zero, ri], axis=1),
        ],
        axis=0,
    )
    li = li_ref[...]
    for t in range(tiles):
        copies[t].wait()
        pairs = tile // 256
        stacked = jnp.concatenate(
            [held[t, :, c * 256 : (c + 1) * 256] for c in range(pairs)], axis=0
        )
        first = lax.dot_general(
            stacked, pair, (((1,), (1,)), ((), ())), preferred_element_type=F32
        ).astype(BF16)
        first = jnp.concatenate(
            [first[c * 128 : (c + 1) * 128] for c in range(pairs)], axis=1
        )
        second = matmul(li, first)
        for p in range(tile // 128):
            turned[pl.ds(t * (tile // 128) + p, 128, stride=BLOCKS), :] = second[
                :, p * 128 : (p + 1) * 128
            ]
    parts = []
    for part in range(4):
        half = 1 - part // 2
        for r in range(32):
            if outs == 1:
                to = part * 32 + r
                row = to * BLOCKS
            else:
                at = part % 2 * 32 + r
                to = half * 64 + at
                row = pl.multiple_of((2 * at + (xl_ref[0] ^ half)) * BLOCKS, 8)
            packed[to] = turned[pl.ds(row, BLOCKS), :].astype(BF16)
        if outs == 1:
            here, there = part * 32, o_refs[0].at[pl.ds(part * 32, 32)]
        else:
            at = part % 2 * 32
            here, there = half * 64 + at, o_refs[half].at[pl.ds(at, 32)]
        parts.append(
            pltpu.make_async_copy(packed.at[pl.ds(here, 32)], there, out_sems.at[part])
        )
        parts[-1].start()
    for copy in parts:
        copy.wait()


def inner(weights, matrix, xl, li, ri, cuts, after=()):
    hbm = pl.BlockSpec(memory_space=pltpu.HBM)
    return pl.pallas_call(
        functools.partial(inner_kernel, matrix, cuts),
        in_specs=[pl.BlockSpec(memory_space=pltpu.SMEM), hbm, WHOLE, WHOLE]
        + [ORDER] * len(after),
        out_specs=[hbm] * cuts,
        out_shape=[blocks_of(128 // cuts)] * cuts,
        scratch_shapes=[
            pltpu.VMEM((4, 128, WIDTH // 4), BF16),
            pltpu.VMEM((128 * BLOCKS, 128), F32),
            pltpu.VMEM((128, BLOCKS, 128), BF16),
            pltpu.SemaphoreType.DMA((4,)),
            pltpu.SemaphoreType.DMA((4,)),
        ],
        compiler_params=pltpu.CompilerParams(vmem_limit_bytes=INNER_VMEM),
        cost_estimate=cost(4 * 128 * 128 * WIDTH, 2),
        name=f"inner{matrix}",
    )(xl, weights, li, ri, *after)


def mix_blocks(refs, rows, ro):
    columns = jnp.concatenate(
        [
            jnp.concatenate([ref[at].astype(F32) for ref, at in zip(refs, where)], axis=0)
            for where in rows
        ],
        axis=1,
    )
    return matmul(ro, columns.astype(BF16))


def right_kernel(ro_ref, *refs):
    sources, (o_ref, packed, sems) = refs[:4], refs[-3:]
    ro = ro_ref[...]
    parts = []
    for first in range(0, 64, 4):
        rows = range(first, first + 4)
        mixed = mix_blocks(sources, [(r,) * 4 for r in rows], ro)
        for at, r in enumerate(rows):
            lanes = slice(at * 128, at * 128 + 128)
            packed[2 * r] = mixed[:BLOCKS, lanes].astype(BF16)
            packed[2 * r + 1] = mixed[BLOCKS:, lanes].astype(BF16)
        if first % 16 == 12:
            done = pl.ds(2 * (first - 12), 32)
            parts.append(
                pltpu.make_async_copy(
                    packed.at[done], o_ref.at[done], sems.at[first // 16]
                )
            )
            parts[-1].start()
    for copy in parts:
        copy.wait()


def right(sources, ro, after=()):
    return pl.pallas_call(
        right_kernel,
        in_specs=[WHOLE] * 5 + [ORDER] * len(after),
        out_specs=pl.BlockSpec(memory_space=pltpu.HBM),
        out_shape=blocks_of(128),
        scratch_shapes=[
            pltpu.VMEM((128, BLOCKS, 128), BF16),
            pltpu.SemaphoreType.DMA((4,)),
        ],
        compiler_params=pltpu.CompilerParams(vmem_limit_bytes=VMEM),
        cost_estimate=cost(1153 * 10**6 * 20, 3),
        name="right",
    )(ro, *sources, *after)


def both_kernel(ro_ref, lo_ref, own_ref, other_ref, *refs):
    o_refs, turned = refs[-3:-1], refs[-1]
    ro = ro_ref[...]
    sources = (own_ref, own_ref, other_ref, other_ref)
    stride = 72
    for first in range(0, 64, 4):
        rows = range(first, first + 4)
        mixed = mix_blocks(sources, [(2 * r, 2 * r + 1) * 2 for r in rows], ro)
        for at, r in enumerate(rows):
            turned[pl.ds(r, 2 * BLOCKS, stride=stride), :] = mixed[
                :, at * 128 : at * 128 + 128
            ]
    lo = lo_ref[...]
    for half, ref in enumerate(o_refs):
        for first in range(0, BLOCKS, 14):
            x = jnp.concatenate(
                [
                    turned[
                        (half * BLOCKS + p) * stride : (half * BLOCKS + p) * stride + 64, :
                    ].astype(BF16)
                    for p in range(first, first + 14)
                ],
                axis=1,
            )
            ref[:, first * 128 : (first + 14) * 128] = matmul(lo, x).astype(BF16)


def both(own, other, ro, lo, after=()):
    return pl.pallas_call(
        both_kernel,
        in_specs=[WHOLE] * 4 + [ORDER] * len(after),
        out_specs=[WHOLE] * 2,
        out_shape=[jax.ShapeDtypeStruct((64, WIDTH), BF16)] * 2,
        scratch_shapes=[pltpu.VMEM((2 * BLOCKS * 72, 128), F32)],
        compiler_params=pltpu.CompilerParams(vmem_limit_bytes=VMEM),
        cost_estimate=cost(10 * 64 * BLOCKS * WIDTH, 3),
        name="both",
    )(ro, lo, own, other, *after)


def block_scales(values, first, held):
    lanes = lax.broadcasted_iota(jnp.int32, held.shape, 1)
    for p in range(values.shape[1] // 128):
        block = jnp.abs(values[:, p * 128 : (p + 1) * 128].astype(F32))
        largest = jnp.max(block, axis=1, keepdims=True) / 1.5
        held = jnp.where(lanes == first + p, largest, held)
    return held


OUTPUTS = [
    jax.ShapeDtypeStruct((3, 2, 64, WIDTH), BF16),
    jax.ShapeDtypeStruct((3, 2, BLOCKS, 64), F32),
]


def last_kernel(lo_ref, x_ref, *refs):
    o_ref, s_ref, turned, held = refs[-4:]
    step = pl.program_id(0)
    tile = o_ref.shape[3]
    stride = 136

    @pl.when(step == 0)
    def _():
        for k in range(64):
            for half in range(2):
                turned[pl.ds(half * 64 + k, BLOCKS, stride=stride), :] = x_ref[
                    2 * k + half
                ].astype(F32)

    first = step * (tile // 128)
    x = jnp.concatenate(
        [
            turned[pl.ds(pl.multiple_of((first + p) * stride, 8), 128), :].astype(BF16)
            for p in range(tile // 128)
        ],
        axis=1,
    )
    values = matmul(lo_ref[...], x).astype(BF16)
    o_ref[...] = values.reshape(1, 2, 64, tile)
    scales = block_scales(values, first, held[...])
    held[...] = scales
    flat = scales.T
    s_ref[0, 0] = flat[:BLOCKS, :64]
    s_ref[0, 1] = flat[:BLOCKS, 64:]


def last(x, lo, matrix, rotated, scales):
    tile = 1792
    return pl.pallas_call(
        last_kernel,
        grid=(WIDTH // tile,),
        in_specs=[
            pl.BlockSpec((128, 128), lambda i: (0, 0)),
            pl.BlockSpec((128, BLOCKS, 128), lambda i: (0, 0, 0)),
            ORDER,
            ORDER,
        ],
        out_specs=[
            pl.BlockSpec((1, 2, 64, tile), lambda i: (matrix, 0, 0, i)),
            pl.BlockSpec((1, 2, BLOCKS, 64), lambda i: (matrix, 0, 0, 0)),
        ],
        out_shape=OUTPUTS,
        scratch_shapes=[
            pltpu.VMEM((BLOCKS * 136, 128), F32),
            pltpu.VMEM((128, 128), F32),
        ],
        input_output_aliases={2: 0, 3: 1},
        compiler_params=pltpu.CompilerParams(vmem_limit_bytes=VMEM),
        cost_estimate=cost(2 * 128 * 128 * WIDTH, 2),
        name=f"last{matrix}",
    )(lo, x, rotated, scales)


def place_kernel(flip_ref, own_ref, other_ref, o_ref, s_ref, held):
    tile = o_ref.shape[3]
    lanes = pl.program_id(1) * (tile // 128)

    def put(ref):
        values = ref[...]
        o_ref[...] = values.reshape(1, 1, 64, tile)
        scales = block_scales(values, lanes, held[...])
        held[...] = scales
        s_ref[0, 0] = scales.T[:BLOCKS]

    pl.when(pl.program_id(0) == flip_ref[0])(lambda: put(own_ref))
    pl.when(pl.program_id(0) != flip_ref[0])(lambda: put(other_ref))


def place(own, other, flip):
    tile = 1792
    return pl.pallas_call(
        place_kernel,
        grid_spec=pltpu.PrefetchScalarGridSpec(
            num_scalar_prefetch=1,
            grid=(2, WIDTH // tile),
            in_specs=[pl.BlockSpec((64, tile), lambda h, i, flip: (0, i))] * 2,
            out_specs=[
                pl.BlockSpec((1, 1, 64, tile), lambda h, i, flip: (0, h, 0, i)),
                pl.BlockSpec((1, 1, BLOCKS, 64), lambda h, i, flip: (0, h, 0, 0)),
            ],
            scratch_shapes=[pltpu.VMEM((64, 128), F32)],
        ),
        out_shape=OUTPUTS,
        compiler_params=pltpu.CompilerParams(vmem_limit_bytes=VMEM),
        cost_estimate=cost(128 * WIDTH, 2),
        name="place",
    )(flip, own, other)


def gate(x, after):
    return pl.pallas_call(
        lambda *refs: None,
        in_specs=[ORDER] * (1 + len(after)),
        out_specs=ORDER,
        out_shape=jax.ShapeDtypeStruct(x.shape, x.dtype),
        input_output_aliases={0: 0},
        cost_estimate=pl.CostEstimate(flops=128, bytes_accessed=1024, transcendentals=0),
        name="gate",
    )(x, *after)


def swap(x, axis):
    return lax.ppermute(x, axis, [(0, 1), (1, 0)])


def exchange(x):
    return lax.all_to_all(x, (XH, Y, Z, XL), split_axis=0, concat_axis=0, tiled=True)


def local(weights, left_outer, left_inner, right_outer, right_inner):
    xl, core = lax.axis_index(XL), lax.axis_index(CORE)
    flip = jnp.full((1,), xl, jnp.int32)

    zero = jnp.zeros_like(left_outer)
    lo12 = jnp.concatenate(
        [
            jnp.concatenate([left_outer, zero], axis=1),
            jnp.concatenate([zero, left_outer], axis=1),
        ],
        axis=0,
    )

    ro = right_outer.reshape(2, 2, BLOCKS, 2, 2, BLOCKS)
    ro = jnp.where(core == 0, ro[:, 0], ro[:, 1, :, :, ::-1])
    ro = ro.transpose(0, 1, 3, 2, 4)
    ro0 = jnp.where(xl == 0, ro, ro[::-1]).reshape(2 * BLOCKS, 4 * BLOCKS)
    ro12 = jnp.where(xl == 0, ro, ro[:, :, :, ::-1]).reshape(2 * BLOCKS, 4 * BLOCKS)

    keep1, send1 = inner(weights, 1, flip, left_inner, right_inner, 2)
    (sent0,) = inner(weights, 0, flip, left_inner, right_inner, 1, [keep1])
    keep2, send2 = inner(weights, 2, flip, left_inner, right_inner, 2, [sent0])
    came0 = exchange(sent0)

    came1 = swap(send1, XL)
    keep1 = gate(keep1, [came1])
    sent1 = right([keep1, came1, swap(keep1, CORE), swap(came1, CORE)], ro12, [keep2])
    came2 = swap(send2, XL)
    keep2 = gate(keep2, [came2])

    came0 = gate(came0, [sent1, came2])
    own0, send0 = both(came0, swap(came0, CORE), ro0, left_outer)
    rotated, scales = place(own0, swap(send0, XL), flip)
    sent2 = right([keep2, came2, swap(keep2, CORE), swap(came2, CORE)], ro12, [scales])
    rotated, scales = last(exchange(sent1), lo12, 1, rotated, scales)
    rotated, scales = last(exchange(sent2), lo12, 2, rotated, scales)
    return rotated, scales.transpose(0, 1, 3, 2)


def solution(mesh):
    fine = Mesh(np.asarray(mesh.devices).reshape(SIZES), AXES)
    row, col = (XH, Y, Z), (XL, CORE)
    return jax.shard_map(
        local,
        mesh=fine,
        in_specs=(P(None, row, col), P(), P(), P(), P()),
        out_specs=(P(None, row, None, col), P(None, row, None, col)),
        check_vma=False,
    )
```

```python
import functools

import jax
import jax.numpy as jnp
import numpy as np
from jax import lax
from jax.experimental import pallas as pl
from jax.experimental.pallas import tpu as pltpu
from jax.sharding import Mesh
from jax.sharding import PartitionSpec as P

BF16 = jnp.bfloat16
F32 = jnp.float32
XH, Y, Z, XL, CORE = "xh", "y", "z", "xl", "core"
AXES = (XH, Y, Z, XL, CORE)
SIZES = (2, 4, 8, 2, 2)
WIDTH = 7168
BLOCKS = 56
VMEM = 24 * 1024 * 1024
INNER_VMEM = 60 * 1024 * 1024
MICROS = 20
WHOLE = pl.BlockSpec(memory_space=pltpu.VMEM)
ORDER = pl.BlockSpec(memory_space=pl.ANY)


def matmul(left, right):
    return jnp.dot(left, right, preferred_element_type=F32)


def blocks_of(count):
    return jax.ShapeDtypeStruct((count, BLOCKS, 128), BF16)


def cost(flops, passes):
    return pl.CostEstimate(
        flops=flops, bytes_accessed=passes * 128 * WIDTH * 2, transcendentals=0
    )


def inner_kernel(matrices, outs, place_ref, w_ref, li_ref, ri_ref, *refs):
    o_refs, (held, turned, packed, sems, out_sems) = refs[-5 - outs : -5], refs[-5:]
    tiles = 4
    tile = WIDTH // tiles
    copies = [
        pltpu.make_async_copy(
            w_ref.at[matrix, :, pl.ds(t * tile, tile)],
            held.at[at * tiles + t],
            sems.at[at * tiles + t],
        )
        for at, matrix in enumerate(matrices)
        for t in range(tiles)
    ]
    for copy in copies:
        copy.start()
    ri = ri_ref[...]
    zero = jnp.zeros_like(ri)
    pair = jnp.concatenate(
        [
            jnp.concatenate([ri, zero], axis=1),
            jnp.concatenate([zero, ri], axis=1),
        ],
        axis=0,
    )
    li = li_ref[...]
    parts = []
    for place in range(len(matrices)):
        for t in range(tiles):
            which = place * tiles + t
            copies[which].wait()
            pairs = tile // 256
            stacked = jnp.concatenate(
                [held[which, :, c * 256 : (c + 1) * 256] for c in range(pairs)], axis=0
            )
            first = lax.dot_general(
                stacked, pair, (((1,), (1,)), ((), ())), preferred_element_type=F32
            ).astype(BF16)
            first = jnp.concatenate(
                [first[c * 128 : (c + 1) * 128] for c in range(pairs)], axis=1
            )
            second = matmul(li, first)
            for p in range(tile // 128):
                turned[pl.ds(t * (tile // 128) + p, 128, stride=BLOCKS), :] = second[
                    :, p * 128 : (p + 1) * 128
                ]
        for part in range(4):
            half = 1 - part // 2
            for r in range(32):
                if outs == 1:
                    to = part * 32 + r
                    row = to * BLOCKS
                else:
                    to = half * 64 + part % 2 * 32 + r
                    at = (place_ref[0] ^ (part % 2)) * 32 + r
                    row = pl.multiple_of((2 * at + (place_ref[1] ^ half)) * BLOCKS, 8)
                packed[place, to] = turned[pl.ds(row, BLOCKS), :].astype(BF16)
            if outs == 1:
                here, there = part * 32, o_refs[0].at[pl.ds(part * 32, 32), place]
            else:
                at = part % 2 * 32
                here, there = half * 64 + at, o_refs[half].at[pl.ds(at, 32)]
            parts.append(
                pltpu.make_async_copy(
                    packed.at[place, pl.ds(here, 32)], there, out_sems.at[len(parts)]
                )
            )
            parts[-1].start()
    for copy in parts:
        copy.wait()


def inner(weights, matrices, where, li, ri, shapes, after=()):
    hbm = pl.BlockSpec(memory_space=pltpu.HBM)
    count = len(matrices)
    return pl.pallas_call(
        functools.partial(inner_kernel, matrices, len(shapes)),
        in_specs=[pl.BlockSpec(memory_space=pltpu.SMEM), hbm, WHOLE, WHOLE]
        + [ORDER] * len(after),
        out_specs=[hbm] * len(shapes),
        out_shape=shapes,
        scratch_shapes=[
            pltpu.VMEM((4 * count, 128, WIDTH // 4), BF16),
            pltpu.VMEM((128 * BLOCKS, 128), F32),
            pltpu.VMEM((count, 128, BLOCKS, 128), BF16),
            pltpu.SemaphoreType.DMA((4 * count,)),
            pltpu.SemaphoreType.DMA((4 * count,)),
        ],
        compiler_params=pltpu.CompilerParams(vmem_limit_bytes=INNER_VMEM),
        cost_estimate=cost(4 * 128 * 128 * WIDTH, 2),
        name=f"inner{matrices[0]}",
    )(where, weights, li, ri, *after)


def mix_blocks(refs, rows, ro):
    columns = jnp.concatenate(
        [
            jnp.concatenate([ref[at].astype(F32) for ref, at in zip(refs, where)], axis=0)
            for where in rows
        ],
        axis=1,
    )
    return matmul(ro, columns.astype(BF16))


def right_kernel(ro_ref, *refs):
    sources, (packed, sems) = refs[:4], refs[-2:]
    o_refs = refs[-6:-2]
    ro = ro_ref[...]
    copies = []
    for first in range(0, 64, 4):
        rows = range(first, first + 4)
        mixed = mix_blocks(sources, [(r,) * 4 for r in rows], ro)
        for at, r in enumerate(rows):
            lanes = slice(at * 128, at * 128 + 128)
            for half in range(2):
                block = mixed[half * BLOCKS : (half + 1) * BLOCKS, lanes]
                packed[r // 32 * 2 + half, r % 32] = block.astype(BF16)
        if first % 32 == 28:
            for to in (first // 32 * 2, first // 32 * 2 + 1):
                copies.append(pltpu.make_async_copy(packed.at[to], o_refs[to], sems.at[to]))
                copies[-1].start()
    for copy in copies:
        copy.wait()


def right(sources, ro, after=()):
    return pl.pallas_call(
        right_kernel,
        in_specs=[WHOLE] * 5 + [ORDER] * len(after),
        out_specs=[pl.BlockSpec(memory_space=pltpu.HBM)] * 4,
        out_shape=[blocks_of(32)] * 4,
        scratch_shapes=[
            pltpu.VMEM((4, 32, BLOCKS, 128), BF16),
            pltpu.SemaphoreType.DMA((4,)),
        ],
        compiler_params=pltpu.CompilerParams(vmem_limit_bytes=VMEM),
        cost_estimate=cost(1153 * 10**6 * MICROS, 3),
        name="right",
    )(ro, *sources, *after)


def join_kernel(*refs):
    o_ref, packed, sems = refs[-3:]
    copies = []
    for part in range(4):
        rows = pl.ds(part * 8, 8)
        for row in range(part * 8, part * 8 + 8):
            for at, ref in enumerate(refs[:4]):
                packed[row, at] = ref[row]
        copies.append(
            pltpu.make_async_copy(packed.at[rows], o_ref.at[rows], sems.at[part])
        )
        copies[-1].start()
    for copy in copies:
        copy.wait()


def join(pieces):
    return pl.pallas_call(
        join_kernel,
        in_specs=[WHOLE] * 4,
        out_specs=pl.BlockSpec(memory_space=pltpu.HBM),
        out_shape=jax.ShapeDtypeStruct((32, 4, BLOCKS, 128), BF16),
        scratch_shapes=[
            pltpu.VMEM((32, 4, BLOCKS, 128), BF16),
            pltpu.SemaphoreType.DMA((4,)),
        ],
        compiler_params=pltpu.CompilerParams(vmem_limit_bytes=VMEM),
        cost_estimate=cost(0, 2),
        name="join",
    )(*pieces)


def both_kernel(matrix, ro_ref, lo_ref, own_ref, other_ref, *refs):
    o_refs, turned = refs[-3:-1], refs[-1]
    ro = ro_ref[...]
    sources = (own_ref, own_ref, other_ref, other_ref)
    stride = 72
    for first in range(0, 64, 4):
        rows = range(first, first + 4)
        where = [((2 * r, 0), (2 * r + 1, 0)) * 2 for r in rows]
        mixed = mix_blocks(sources, where, ro)
        for at, r in enumerate(rows):
            turned[pl.ds(r, 2 * BLOCKS, stride=stride), :] = mixed[
                :, at * 128 : at * 128 + 128
            ]
    lo = lo_ref[...]
    for half, ref in enumerate(o_refs):
        for first in range(0, BLOCKS, 14):
            x = jnp.concatenate(
                [
                    turned[
                        (half * BLOCKS + p) * stride : (half * BLOCKS + p) * stride + 64, :
                    ].astype(BF16)
                    for p in range(first, first + 14)
                ],
                axis=1,
            )
            ref[:, first * 128 : (first + 14) * 128] = matmul(lo, x).astype(BF16)


def both(own, other, matrix, ro, lo):
    fixed = lambda shape: pl.BlockSpec(shape, lambda i: (0,) * len(shape))
    blocks = pl.BlockSpec((128, 1, BLOCKS, 128), lambda i: (0, matrix, 0, 0))
    return pl.pallas_call(
        functools.partial(both_kernel, matrix),
        grid=(1,),
        in_specs=[fixed(ro.shape), fixed(lo.shape), blocks, blocks],
        out_specs=[fixed((64, WIDTH))] * 2,
        out_shape=[jax.ShapeDtypeStruct((64, WIDTH), BF16)] * 2,
        scratch_shapes=[pltpu.VMEM((2 * BLOCKS * 72, 128), F32)],
        compiler_params=pltpu.CompilerParams(vmem_limit_bytes=VMEM),
        cost_estimate=cost(10 * 64 * BLOCKS * WIDTH, 3),
        name=f"both{matrix}",
    )(ro, lo, own, other)


def block_scales(values, first, held):
    lanes = lax.broadcasted_iota(jnp.int32, held.shape, 1)
    for p in range(values.shape[1] // 128):
        block = jnp.abs(values[:, p * 128 : (p + 1) * 128].astype(F32))
        largest = jnp.max(block, axis=1, keepdims=True) / 1.5
        held = jnp.where(lanes == first + p, largest, held)
    return held


OUTPUTS = [
    jax.ShapeDtypeStruct((3, 2, 64, WIDTH), BF16),
    jax.ShapeDtypeStruct((3, 2, BLOCKS, 64), F32),
]


def last_kernel(lo_ref, x_ref, *refs):
    o_ref, s_ref, turned, held = refs[-4:]
    step = pl.program_id(0)
    tile = o_ref.shape[3]
    stride = 136

    @pl.when(step == 0)
    def _():
        for row in range(128):
            turned[pl.ds(row, BLOCKS, stride=stride), :] = x_ref[row].astype(F32)

    first = step * (tile // 128)
    x = jnp.concatenate(
        [
            turned[pl.ds(pl.multiple_of((first + p) * stride, 8), 128), :].astype(BF16)
            for p in range(tile // 128)
        ],
        axis=1,
    )
    values = matmul(lo_ref[...], x).astype(BF16)
    o_ref[...] = values.reshape(1, 2, 64, tile)
    scales = block_scales(values, first, held[...])
    held[...] = scales
    flat = scales.T
    s_ref[0, 0] = flat[:BLOCKS, :64]
    s_ref[0, 1] = flat[:BLOCKS, 64:]


def last(x, lo, matrix, rotated, scales):
    tile = 1792
    return pl.pallas_call(
        last_kernel,
        grid=(WIDTH // tile,),
        in_specs=[
            pl.BlockSpec((128, 128), lambda i: (0, 0)),
            pl.BlockSpec((128, BLOCKS, 128), lambda i: (0, 0, 0)),
            ORDER,
            ORDER,
        ],
        out_specs=[
            pl.BlockSpec((1, 2, 64, tile), lambda i: (matrix, 0, 0, i)),
            pl.BlockSpec((1, 2, BLOCKS, 64), lambda i: (matrix, 0, 0, 0)),
        ],
        out_shape=OUTPUTS,
        scratch_shapes=[
            pltpu.VMEM((BLOCKS * 136, 128), F32),
            pltpu.VMEM((128, 128), F32),
        ],
        input_output_aliases={2: 0, 3: 1},
        compiler_params=pltpu.CompilerParams(vmem_limit_bytes=VMEM),
        cost_estimate=cost(2 * 128 * 128 * WIDTH, 2),
        name=f"last{matrix}",
    )(lo, x, rotated, scales)


def place_kernel(half_ref, x_ref, *refs):
    o_ref, s_ref, held = refs[-3:]
    tile = o_ref.shape[3]
    values = x_ref[...]
    o_ref[...] = values.reshape(1, 1, 64, tile)
    scales = block_scales(values, pl.program_id(0) * (tile // 128), held[...])
    held[...] = scales
    s_ref[0, 0] = scales.T[:BLOCKS]


def place(x, half, matrix, into=()):
    tile = 1792
    return pl.pallas_call(
        place_kernel,
        grid_spec=pltpu.PrefetchScalarGridSpec(
            num_scalar_prefetch=1,
            grid=(WIDTH // tile,),
            in_specs=[pl.BlockSpec((64, tile), lambda i, half: (0, i))]
            + [ORDER] * len(into),
            out_specs=[
                pl.BlockSpec((1, 1, 64, tile), lambda i, half: (matrix, half[0], 0, i)),
                pl.BlockSpec((1, 1, BLOCKS, 64), lambda i, half: (matrix, half[0], 0, 0)),
            ],
            scratch_shapes=[pltpu.VMEM((64, 128), F32)],
        ),
        out_shape=OUTPUTS,
        input_output_aliases={2: 0, 3: 1} if into else {},
        compiler_params=pltpu.CompilerParams(vmem_limit_bytes=VMEM),
        cost_estimate=cost(64 * WIDTH, 1),
        name=f"place{matrix}",
    )(half, x, *into)


def gate(x, after):
    return pl.pallas_call(
        lambda *refs: None,
        in_specs=[ORDER] * (1 + len(after)),
        out_specs=ORDER,
        out_shape=jax.ShapeDtypeStruct(x.shape, x.dtype),
        input_output_aliases={0: 0},
        cost_estimate=pl.CostEstimate(flops=128, bytes_accessed=1024, transcendentals=0),
        name="gate",
    )(x, *after)


def swap(x, axis):
    return lax.ppermute(x, axis, [(0, 1), (1, 0)])


def local(weights, left_outer, left_inner, right_outer, right_inner):
    xh, xl, core = lax.axis_index(XH), lax.axis_index(XL), lax.axis_index(CORE)
    where = jnp.stack([xh, xl]).astype(jnp.int32)
    own_half = where[1:]

    lo = left_outer.reshape(64, 2, 32)
    lo = jnp.where(xh == 0, lo, lo[:, ::-1]).transpose(0, 2, 1)
    same = jnp.eye(2, dtype=BF16)
    same = jnp.where(xl == 0, same, same[::-1])
    lo2 = lo.reshape(1, 64, 32, 2, 1) * same.reshape(2, 1, 1, 1, 2)
    lo2 = lo2.reshape(128, 128)

    ro = right_outer.reshape(2, 2, BLOCKS, 2, 2, BLOCKS)
    ro = jnp.where(core == 0, ro[:, 0], ro[:, 1, :, :, ::-1])
    ro = ro.transpose(0, 1, 3, 2, 4)
    ro01 = jnp.where(xl == 0, ro, ro[::-1]).reshape(2 * BLOCKS, 4 * BLOCKS)
    ro2 = jnp.where(xl == 0, ro, ro[::-1, :, :, ::-1]).reshape(2 * BLOCKS, 4 * BLOCKS)

    sent01_shape = jax.ShapeDtypeStruct((128, 2, BLOCKS, 128), BF16)
    (sent01,) = inner(weights, (0, 1), where, left_inner, right_inner, [sent01_shape])
    came01 = lax.all_to_all(sent01, (XH, Y, Z, XL), 0, 0, tiled=True)

    keep2, send2 = inner(
        weights, (2,), where, left_inner, right_inner, [blocks_of(64)] * 2, [sent01]
    )
    came2 = swap(send2, XL)
    keep2 = gate(keep2, [came2])
    planes = right([keep2, came2, swap(keep2, CORE), swap(came2, CORE)], ro2)
    planes = [planes[0]] + [
        lax.ppermute(planes[d], (XH, XL), [(i, i ^ d) for i in range(4)])
        for d in range(1, 4)
    ]
    sent2 = join(planes)
    came01 = gate(came01, [sent2])
    came2 = lax.all_to_all(sent2, (Y, Z), 0, 0, tiled=True)

    other01 = swap(came01, CORE)
    own0, send0 = both(came01, other01, 0, ro01, left_outer)
    own1, send1 = both(came01, other01, 1, ro01, left_outer)
    outputs = place(own0, own_half, 0)
    outputs = place(own1, own_half, 1, outputs)
    outputs = place(swap(send0, XL), 1 - own_half, 0, outputs)
    outputs = place(swap(send1, XL), 1 - own_half, 1, outputs)
    rotated, scales = last(came2.reshape(128, BLOCKS, 128), lo2, 2, *outputs)
    return rotated, scales.transpose(0, 1, 3, 2)


def solution(mesh):
    fine = Mesh(np.asarray(mesh.devices).reshape(SIZES), AXES)
    row, col = (XH, Y, Z), (XL, CORE)
    return jax.shard_map(
        local,
        mesh=fine,
        in_specs=(P(None, row, col), P(), P(), P(), P()),
        out_specs=(P(None, row, None, col), P(None, row, None, col)),
        check_vma=False,
    )
```

```python
import functools

import jax
import jax.numpy as jnp
import numpy as np
from jax import lax
from jax.experimental import pallas as pl
from jax.experimental.pallas import tpu as pltpu
from jax.sharding import Mesh
from jax.sharding import PartitionSpec as P

BF16 = jnp.bfloat16
F32 = jnp.float32
XH, Y, Z, XL, CORE = "xh", "y", "z", "xl", "core"
AXES = (XH, Y, Z, XL, CORE)
SIZES = (2, 4, 8, 2, 2)
WIDTH = 7168
BLOCKS = 56
MIB = 1024 * 1024
VMEM = 24 * MIB
INNER_VMEM = 60 * MIB
MICROS = 20
PITCH = BLOCKS + 1
WHOLE = pl.BlockSpec(memory_space=pltpu.VMEM)
ORDER = pl.BlockSpec(memory_space=pl.ANY)


def matmul(left, right):
    return jnp.dot(left, right, preferred_element_type=F32)


def blocks_of(count):
    return jax.ShapeDtypeStruct((count, BLOCKS, 128), BF16)


def cost(flops, passes):
    return pl.CostEstimate(
        flops=flops, bytes_accessed=passes * 128 * WIDTH * 2, transcendentals=0
    )


def inner_kernel(matrices, outs, place_ref, w_ref, li_ref, ri_ref, *refs):
    o_refs, (held, turned, packed, sems, out_sems) = refs[-5 - outs : -5], refs[-5:]
    tiles = 4
    tile = WIDTH // tiles
    copies = [
        pltpu.make_async_copy(
            w_ref.at[matrix, :, pl.ds(t * tile, tile)],
            held.at[at * tiles + t],
            sems.at[at * tiles + t],
        )
        for at, matrix in enumerate(matrices)
        for t in range(tiles)
    ]
    for copy in copies:
        copy.start()
    ri = ri_ref[...]
    zero = jnp.zeros_like(ri)
    pair = jnp.concatenate(
        [
            jnp.concatenate([ri, zero], axis=1),
            jnp.concatenate([zero, ri], axis=1),
        ],
        axis=0,
    )
    li = li_ref[...]
    parts = []
    for place in range(len(matrices)):
        for t in range(tiles):
            which = place * tiles + t
            copies[which].wait()
            pairs = tile // 256
            stacked = jnp.concatenate(
                [held[which, :, c * 256 : (c + 1) * 256] for c in range(pairs)], axis=0
            )
            first = lax.dot_general(
                stacked, pair, (((1,), (1,)), ((), ())), preferred_element_type=F32
            ).astype(BF16)
            first = jnp.concatenate(
                [first[c * 128 : (c + 1) * 128] for c in range(pairs)], axis=1
            )
            second = matmul(li, first)
            for p in range(tile // 128):
                turned[pl.ds(t * (tile // 128) + p, 128, stride=PITCH), :] = second[
                    :, p * 128 : (p + 1) * 128
                ]
        for part in range(4):
            half = 1 - part // 2
            for r in range(32):
                if outs == 1:
                    to = part * 32 + r
                    row = to * PITCH
                else:
                    to = half * 64 + part % 2 * 32 + r
                    at = (place_ref[0] ^ (part % 2)) * 32 + r
                    row = (2 * at + (place_ref[1] ^ half)) * PITCH
                packed[place, to] = turned[pl.ds(row, BLOCKS), :].astype(BF16)
            if outs == 1:
                here, there = part * 32, o_refs[0].at[pl.ds(part * 32, 32), place]
            else:
                at = part % 2 * 32
                here, there = half * 64 + at, o_refs[half].at[pl.ds(at, 32)]
            parts.append(
                pltpu.make_async_copy(
                    packed.at[place, pl.ds(here, 32)], there, out_sems.at[len(parts)]
                )
            )
            parts[-1].start()
    for copy in parts:
        copy.wait()


def inner(weights, matrices, where, li, ri, shapes, after=()):
    hbm = pl.BlockSpec(memory_space=pltpu.HBM)
    count = len(matrices)
    return pl.pallas_call(
        functools.partial(inner_kernel, matrices, len(shapes)),
        in_specs=[pl.BlockSpec(memory_space=pltpu.SMEM), hbm, WHOLE, WHOLE]
        + [ORDER] * len(after),
        out_specs=[hbm] * len(shapes),
        out_shape=shapes,
        scratch_shapes=[
            pltpu.VMEM((4 * count, 128, WIDTH // 4), BF16),
            pltpu.VMEM((128 * PITCH, 128), F32),
            pltpu.VMEM((count, 128, BLOCKS, 128), BF16),
            pltpu.SemaphoreType.DMA((4 * count,)),
            pltpu.SemaphoreType.DMA((4 * count,)),
        ],
        compiler_params=pltpu.CompilerParams(vmem_limit_bytes=INNER_VMEM),
        cost_estimate=cost(4 * 128 * 128 * WIDTH, 2),
        name=f"inner{matrices[0]}",
    )(where, weights, li, ri, *after)


def mix_blocks(refs, rows, ro):
    columns = jnp.concatenate(
        [
            jnp.concatenate([ref[at].astype(F32) for ref, at in zip(refs, where)], axis=0)
            for where in rows
        ],
        axis=1,
    )
    return matmul(ro, columns.astype(BF16))


def right_kernel(ro_ref, *refs):
    sources, (packed, sems) = refs[:4], refs[-2:]
    o_refs = refs[-6:-2]
    ro = ro_ref[...]
    copies = []
    for first in range(0, 64, 4):
        rows = range(first, first + 4)
        mixed = mix_blocks(sources, [(r,) * 4 for r in rows], ro)
        for at, r in enumerate(rows):
            lanes = slice(at * 128, at * 128 + 128)
            for half in range(2):
                block = mixed[half * BLOCKS : (half + 1) * BLOCKS, lanes]
                packed[r // 32 * 2 + half, r % 32] = block.astype(BF16)
        if first % 32 == 28:
            for to in (first // 32 * 2, first // 32 * 2 + 1):
                copies.append(pltpu.make_async_copy(packed.at[to], o_refs[to], sems.at[to]))
                copies[-1].start()
    for copy in copies:
        copy.wait()


def right(sources, ro, after=()):
    return pl.pallas_call(
        right_kernel,
        in_specs=[WHOLE] * 5 + [ORDER] * len(after),
        out_specs=[pl.BlockSpec(memory_space=pltpu.HBM)] * 4,
        out_shape=[blocks_of(32)] * 4,
        scratch_shapes=[
            pltpu.VMEM((4, 32, BLOCKS, 128), BF16),
            pltpu.SemaphoreType.DMA((4,)),
        ],
        compiler_params=pltpu.CompilerParams(vmem_limit_bytes=VMEM),
        cost_estimate=cost(1153 * 10**6 * MICROS, 3),
        name="right",
    )(ro, *sources, *after)


def join_kernel(*refs):
    o_ref, packed, sems = refs[-3:]
    copies = []
    for part in range(4):
        rows = pl.ds(part * 8, 8)
        for row in range(part * 8, part * 8 + 8):
            for at, ref in enumerate(refs[:4]):
                packed[row, at] = ref[row]
        copies.append(
            pltpu.make_async_copy(packed.at[rows], o_ref.at[rows], sems.at[part])
        )
        copies[-1].start()
    for copy in copies:
        copy.wait()


def join(pieces):
    return pl.pallas_call(
        join_kernel,
        in_specs=[WHOLE] * 4,
        out_specs=pl.BlockSpec(memory_space=pltpu.HBM),
        out_shape=jax.ShapeDtypeStruct((32, 4, BLOCKS, 128), BF16),
        scratch_shapes=[
            pltpu.VMEM((32, 4, BLOCKS, 128), BF16),
            pltpu.SemaphoreType.DMA((4,)),
        ],
        compiler_params=pltpu.CompilerParams(vmem_limit_bytes=VMEM),
        cost_estimate=cost(0, 2),
        name="join",
    )(*pieces)


def both_kernel(matrix, ro_ref, lo_ref, own_ref, other_ref, *refs):
    o_refs, (held, turned, sems) = refs[-5:-3], refs[-3:]
    arriving = [
        [
            pltpu.make_async_copy(
                ref.at[pl.ds(part * 32, 32), matrix],
                held.at[at, pl.ds(part * 32, 32)],
                sems.at[at, part],
            )
            for at, ref in enumerate((own_ref, other_ref))
        ]
        for part in range(4)
    ]
    for part in arriving:
        for copy in part:
            copy.start()
    ro = ro_ref[...]
    stride = 73
    for first in range(0, 64, 4):
        if first % 16 == 0:
            for copy in arriving[first // 16]:
                copy.wait()
        rows = range(first, first + 4)
        where = [[(at, 2 * r + half) for at in (0, 1) for half in (0, 1)] for r in rows]
        mixed = mix_blocks([held] * 4, where, ro)
        for at, r in enumerate(rows):
            turned[pl.ds(r, 2 * BLOCKS, stride=stride), :] = mixed[
                :, at * 128 : at * 128 + 128
            ]
    lo = lo_ref[...]
    for half, ref in enumerate(o_refs):
        for first in range(0, BLOCKS, 14):
            x = jnp.concatenate(
                [
                    turned[
                        (half * BLOCKS + p) * stride : (half * BLOCKS + p) * stride + 64, :
                    ].astype(BF16)
                    for p in range(first, first + 14)
                ],
                axis=1,
            )
            ref[:, first * 128 : (first + 14) * 128] = matmul(lo, x).astype(BF16)


def both(own, other, matrix, ro, lo):
    hbm = pl.BlockSpec(memory_space=pltpu.HBM)
    return pl.pallas_call(
        functools.partial(both_kernel, matrix),
        in_specs=[WHOLE, WHOLE, hbm, hbm],
        out_specs=[WHOLE] * 2,
        out_shape=[jax.ShapeDtypeStruct((64, WIDTH), BF16)] * 2,
        scratch_shapes=[
            pltpu.VMEM((2, 128, BLOCKS, 128), BF16),
            pltpu.VMEM((2 * BLOCKS * 73, 128), F32),
            pltpu.SemaphoreType.DMA((2, 4)),
        ],
        compiler_params=pltpu.CompilerParams(vmem_limit_bytes=18 * MIB),
        cost_estimate=cost(10 * 64 * BLOCKS * WIDTH, 3),
        name=f"both{matrix}",
    )(ro, lo, own, other)


def block_scales(values, first, held):
    lanes = lax.broadcasted_iota(jnp.int32, held.shape, 1)
    for p in range(values.shape[1] // 128):
        block = jnp.abs(values[:, p * 128 : (p + 1) * 128].astype(F32))
        largest = jnp.max(block, axis=1, keepdims=True) / 1.5
        held = jnp.where(lanes == first + p, largest, held)
    return held


OUTPUTS = [
    jax.ShapeDtypeStruct((3, 2, 64, WIDTH), BF16),
    jax.ShapeDtypeStruct((3, 2, BLOCKS, 64), F32),
]


def last_kernel(lo_ref, x_ref, *refs):
    o_ref, s_ref, turned, held = refs[-4:]
    step = pl.program_id(0)
    tile = o_ref.shape[3]
    stride = 137

    @pl.when(step == 0)
    def _():
        for row in range(128):
            turned[pl.ds(row, BLOCKS, stride=stride), :] = x_ref[row].astype(F32)

    first = step * (tile // 128)
    x = jnp.concatenate(
        [
            turned[pl.ds((first + p) * stride, 128), :].astype(BF16)
            for p in range(tile // 128)
        ],
        axis=1,
    )
    values = matmul(lo_ref[...], x).astype(BF16)
    o_ref[...] = values.reshape(1, 2, 64, tile)
    scales = block_scales(values, first, held[...])
    held[...] = scales
    flat = scales.T
    s_ref[0, 0] = flat[:BLOCKS, :64]
    s_ref[0, 1] = flat[:BLOCKS, 64:]


def last(x, lo, matrix, rotated, scales):
    tile = 1792
    return pl.pallas_call(
        last_kernel,
        grid=(WIDTH // tile,),
        in_specs=[
            pl.BlockSpec((128, 128), lambda i: (0, 0)),
            pl.BlockSpec((128, BLOCKS, 128), lambda i: (0, 0, 0)),
            ORDER,
            ORDER,
        ],
        out_specs=[
            pl.BlockSpec((1, 2, 64, tile), lambda i: (matrix, 0, 0, i)),
            pl.BlockSpec((1, 2, BLOCKS, 64), lambda i: (matrix, 0, 0, 0)),
        ],
        out_shape=OUTPUTS,
        scratch_shapes=[
            pltpu.VMEM((BLOCKS * 137, 128), F32),
            pltpu.VMEM((128, 128), F32),
        ],
        input_output_aliases={2: 0, 3: 1},
        compiler_params=pltpu.CompilerParams(vmem_limit_bytes=12 * MIB),
        cost_estimate=cost(2 * 128 * 128 * WIDTH, 2),
        name=f"last{matrix}",
    )(lo, x, rotated, scales)


def place_kernel(half_ref, x_ref, *refs):
    o_ref, s_ref, held = refs[-3:]
    tile = o_ref.shape[3]
    values = x_ref[...]
    o_ref[...] = values.reshape(1, 1, 64, tile)
    scales = block_scales(values, pl.program_id(0) * (tile // 128), held[...])
    held[...] = scales
    s_ref[0, 0] = scales.T[:BLOCKS]


def place(x, half, matrix, into=()):
    tile = 1792
    return pl.pallas_call(
        place_kernel,
        grid_spec=pltpu.PrefetchScalarGridSpec(
            num_scalar_prefetch=1,
            grid=(WIDTH // tile,),
            in_specs=[pl.BlockSpec((64, tile), lambda i, half: (0, i))]
            + [ORDER] * len(into),
            out_specs=[
                pl.BlockSpec((1, 1, 64, tile), lambda i, half: (matrix, half[0], 0, i)),
                pl.BlockSpec((1, 1, BLOCKS, 64), lambda i, half: (matrix, half[0], 0, 0)),
            ],
            scratch_shapes=[pltpu.VMEM((64, 128), F32)],
        ),
        out_shape=OUTPUTS,
        input_output_aliases={2: 0, 3: 1} if into else {},
        compiler_params=pltpu.CompilerParams(vmem_limit_bytes=6 * MIB),
        cost_estimate=cost(64 * WIDTH, 1),
        name=f"place{matrix}",
    )(half, x, *into)


def gate(x, after):
    return pl.pallas_call(
        lambda *refs: None,
        in_specs=[ORDER] * (1 + len(after)),
        out_specs=ORDER,
        out_shape=jax.ShapeDtypeStruct(x.shape, x.dtype),
        input_output_aliases={0: 0},
        cost_estimate=pl.CostEstimate(flops=128, bytes_accessed=1024, transcendentals=0),
        name="gate",
    )(x, *after)


def swap(x, axis):
    return lax.ppermute(x, axis, [(0, 1), (1, 0)])


def local(weights, left_outer, left_inner, right_outer, right_inner):
    xh, xl, core = lax.axis_index(XH), lax.axis_index(XL), lax.axis_index(CORE)
    where = jnp.stack([xh, xl]).astype(jnp.int32)
    own_half = where[1:]

    lo = left_outer.reshape(64, 2, 32)
    lo = jnp.where(xh == 0, lo, lo[:, ::-1]).transpose(0, 2, 1)
    same = jnp.eye(2, dtype=BF16)
    same = jnp.where(xl == 0, same, same[::-1])
    lo2 = lo.reshape(1, 64, 32, 2, 1) * same.reshape(2, 1, 1, 1, 2)
    lo2 = lo2.reshape(128, 128)

    ro = right_outer.reshape(2, 2, BLOCKS, 2, 2, BLOCKS)
    ro = jnp.where(core == 0, ro[:, 0], ro[:, 1, :, :, ::-1])
    ro = ro.transpose(0, 1, 3, 2, 4)
    ro01 = jnp.where(xl == 0, ro, ro[::-1]).reshape(2 * BLOCKS, 4 * BLOCKS)
    ro2 = jnp.where(xl == 0, ro, ro[::-1, :, :, ::-1]).reshape(2 * BLOCKS, 4 * BLOCKS)

    sent01_shape = jax.ShapeDtypeStruct((128, 2, BLOCKS, 128), BF16)
    nowhere = jnp.zeros((2,), jnp.int32)
    (sent01,) = inner(
        weights, (0, 1), nowhere, left_inner, right_inner, [sent01_shape]
    )
    came01 = lax.all_to_all(sent01, (XH, Y, Z, XL), 0, 0, tiled=True)

    keep2, send2 = inner(
        weights, (2,), where, left_inner, right_inner, [blocks_of(64)] * 2, [sent01]
    )
    came2 = swap(send2, XL)
    planes = right([keep2, came2, swap(keep2, CORE), swap(came2, CORE)], ro2)
    planes = [planes[0]] + [
        lax.ppermute(planes[d], (XH, XL), [(i, i ^ d) for i in range(4)])
        for d in range(1, 4)
    ]
    sent2 = join(planes)
    came01 = gate(came01, [sent2])
    came2 = lax.all_to_all(sent2, (Y, Z), 0, 0, tiled=True)

    other01 = swap(came01, CORE)
    own0, send0 = both(came01, other01, 0, ro01, left_outer)
    own1, send1 = both(came01, other01, 1, ro01, left_outer)
    outputs = place(own0, own_half, 0)
    outputs = place(own1, own_half, 1, outputs)
    outputs = place(swap(send0, XL), 1 - own_half, 0, outputs)
    outputs = last(came2.reshape(128, BLOCKS, 128), lo2, 2, *outputs)
    rotated, scales = place(swap(send1, XL), 1 - own_half, 1, outputs)
    return rotated, scales.transpose(0, 1, 3, 2)


def solution(mesh):
    fine = Mesh(np.asarray(mesh.devices).reshape(SIZES), AXES)
    row, col = (XH, Y, Z), (XL, CORE)
    return jax.shard_map(
        local,
        mesh=fine,
        in_specs=(P(None, row, col), P(), P(), P(), P()),
        out_specs=(P(None, row, None, col), P(None, row, None, col)),
        check_vma=False,
    )
```

```python
import functools

import jax
import jax.numpy as jnp
import numpy as np
from jax import lax
from jax.experimental import pallas as pl
from jax.experimental.pallas import tpu as pltpu
from jax.sharding import Mesh
from jax.sharding import PartitionSpec as P

BF16 = jnp.bfloat16
F32 = jnp.float32
XH, Y, Z, XL, CORE = "xh", "y", "z", "xl", "core"
AXES = (XH, Y, Z, XL, CORE)
SIZES = (2, 4, 8, 2, 2)
WIDTH = 7168
BLOCKS = 56
MIB = 1024 * 1024
VMEM = 24 * MIB
INNER_VMEM = 60 * MIB
MICROS = 20
PITCH = BLOCKS + 1
WHOLE = pl.BlockSpec(memory_space=pltpu.VMEM)
ORDER = pl.BlockSpec(memory_space=pl.ANY)


def matmul(left, right):
    return jnp.dot(left, right, preferred_element_type=F32)


def blocks_of(count):
    return jax.ShapeDtypeStruct((count, BLOCKS, 128), BF16)


def cost(flops, passes):
    return pl.CostEstimate(
        flops=flops, bytes_accessed=passes * 128 * WIDTH * 2, transcendentals=0
    )


def inner_kernel(matrices, outs, *refs):
    if outs == 2:
        place_ref, refs = refs[0], refs[1:]
    w_ref, li_ref, ri_ref = refs[:3]
    o_refs, (held, turned, packed, sems, out_sems) = refs[-5 - outs : -5], refs[-5:]
    tiles = 1
    tile = WIDTH // tiles
    copies = [
        pltpu.make_async_copy(
            w_ref.at[matrix, :, pl.ds(t * tile, tile)],
            held.at[at * tiles + t],
            sems.at[at * tiles + t],
        )
        for at, matrix in enumerate(matrices)
        for t in range(tiles)
    ]
    for copy in copies:
        copy.start()
    ri = ri_ref[...]
    zero = jnp.zeros_like(ri)
    pair = jnp.concatenate(
        [
            jnp.concatenate([ri, zero], axis=1),
            jnp.concatenate([zero, ri], axis=1),
        ],
        axis=0,
    )
    li = li_ref[...]
    parts = []
    for place in range(len(matrices)):
        for t in range(tiles):
            which = place * tiles + t
            copies[which].wait()
            pairs = tile // 256
            stacked = jnp.concatenate(
                [held[which, :, c * 256 : (c + 1) * 256] for c in range(pairs)], axis=0
            )
            first = lax.dot_general(
                stacked, pair, (((1,), (1,)), ((), ())), preferred_element_type=F32
            ).astype(BF16)
            first = jnp.concatenate(
                [first[c * 128 : (c + 1) * 128] for c in range(pairs)], axis=1
            )
            second = matmul(li, first)
            for p in range(tile // 128):
                turned[pl.ds(t * (tile // 128) + p, 128, stride=PITCH), :] = second[
                    :, p * 128 : (p + 1) * 128
                ]
        for part in range(4):
            half = 1 - part // 2
            for r in range(32):
                if outs == 1:
                    to = part * 32 + r
                    row = to * PITCH
                else:
                    to = half * 64 + part % 2 * 32 + r
                    at = (place_ref[0] ^ (part % 2)) * 32 + r
                    row = (2 * at + (place_ref[1] ^ half)) * PITCH
                packed[place, to] = turned[pl.ds(row, BLOCKS), :].astype(BF16)
            if outs == 1:
                here, there = part * 32, o_refs[0].at[pl.ds(part * 32, 32), place]
            else:
                at = part % 2 * 32
                here, there = half * 64 + at, o_refs[half].at[pl.ds(at, 32)]
            parts.append(
                pltpu.make_async_copy(
                    packed.at[place, pl.ds(here, 32)], there, out_sems.at[len(parts)]
                )
            )
            parts[-1].start()
    for copy in parts:
        copy.wait()


def inner(weights, matrices, where, li, ri, shapes, after=()):
    hbm = pl.BlockSpec(memory_space=pltpu.HBM)
    count = len(matrices)
    scalars = [where] if len(shapes) == 2 else []
    return pl.pallas_call(
        functools.partial(inner_kernel, matrices, len(shapes)),
        in_specs=[pl.BlockSpec(memory_space=pltpu.SMEM)] * len(scalars)
        + [hbm, WHOLE, WHOLE]
        + [ORDER] * len(after),
        out_specs=[hbm] * len(shapes),
        out_shape=shapes,
        scratch_shapes=[
            pltpu.VMEM((1 * count, 128, WIDTH // 1), BF16),
            pltpu.VMEM((128 * PITCH, 128), F32),
            pltpu.VMEM((count, 128, BLOCKS, 128), BF16),
            pltpu.SemaphoreType.DMA((1 * count,)),
            pltpu.SemaphoreType.DMA((4 * count,)),
        ],
        compiler_params=pltpu.CompilerParams(vmem_limit_bytes=INNER_VMEM),
        cost_estimate=cost(4 * 128 * 128 * WIDTH, 2),
        name=f"inner{matrices[0]}",
    )(*scalars, weights, li, ri, *after)


def mix_blocks(refs, rows, ro):
    columns = jnp.concatenate(
        [
            jnp.concatenate([ref[at].astype(F32) for ref, at in zip(refs, where)], axis=0)
            for where in rows
        ],
        axis=1,
    )
    return matmul(ro, columns.astype(BF16))


def right_kernel(ro_ref, *refs):
    sources, (packed, sems) = refs[:4], refs[-2:]
    o_refs = refs[-6:-2]
    ro = ro_ref[...]
    copies = []
    for first in range(0, 64, 4):
        rows = range(first, first + 4)
        mixed = mix_blocks(sources, [(r,) * 4 for r in rows], ro)
        for at, r in enumerate(rows):
            lanes = slice(at * 128, at * 128 + 128)
            for half in range(2):
                block = mixed[half * BLOCKS : (half + 1) * BLOCKS, lanes]
                packed[r // 32 * 2 + half, r % 32] = block.astype(BF16)
        if first % 32 == 28:
            for to in (first // 32 * 2, first // 32 * 2 + 1):
                copies.append(pltpu.make_async_copy(packed.at[to], o_refs[to], sems.at[to]))
                copies[-1].start()
    for copy in copies:
        copy.wait()


def right(sources, ro, after=()):
    return pl.pallas_call(
        right_kernel,
        in_specs=[WHOLE] * 5 + [ORDER] * len(after),
        out_specs=[pl.BlockSpec(memory_space=pltpu.HBM)] * 4,
        out_shape=[blocks_of(32)] * 4,
        scratch_shapes=[
            pltpu.VMEM((4, 32, BLOCKS, 128), BF16),
            pltpu.SemaphoreType.DMA((4,)),
        ],
        compiler_params=pltpu.CompilerParams(vmem_limit_bytes=VMEM),
        cost_estimate=cost(1153 * 10**6 * MICROS, 3),
        name="right",
    )(ro, *sources, *after)


def join_kernel(*refs):
    o_ref, packed, sems = refs[-3:]
    copies = []
    for part in range(4):
        rows = pl.ds(part * 8, 8)
        for row in range(part * 8, part * 8 + 8):
            for at, ref in enumerate(refs[:4]):
                packed[row, at] = ref[row]
        copies.append(
            pltpu.make_async_copy(packed.at[rows], o_ref.at[rows], sems.at[part])
        )
        copies[-1].start()
    for copy in copies:
        copy.wait()


def join(pieces):
    return pl.pallas_call(
        join_kernel,
        in_specs=[WHOLE] * 4,
        out_specs=pl.BlockSpec(memory_space=pltpu.HBM),
        out_shape=jax.ShapeDtypeStruct((32, 4, BLOCKS, 128), BF16),
        scratch_shapes=[
            pltpu.VMEM((32, 4, BLOCKS, 128), BF16),
            pltpu.SemaphoreType.DMA((4,)),
        ],
        compiler_params=pltpu.CompilerParams(vmem_limit_bytes=VMEM),
        cost_estimate=cost(0, 2),
        name="join",
    )(*pieces)


def both_kernel(matrix, ro_ref, lo_ref, own_ref, other_ref, *refs):
    o_refs, (held, turned, sems) = refs[-5:-3], refs[-3:]
    arriving = [
        [
            pltpu.make_async_copy(
                ref.at[pl.ds(part * 32, 32), matrix],
                held.at[at, pl.ds(part * 32, 32)],
                sems.at[at, part],
            )
            for at, ref in enumerate((own_ref, other_ref))
        ]
        for part in range(4)
    ]
    for part in arriving:
        for copy in part:
            copy.start()
    ro = ro_ref[...]
    stride = 73
    for first in range(0, 64, 4):
        if first % 16 == 0:
            for copy in arriving[first // 16]:
                copy.wait()
        rows = range(first, first + 4)
        where = [[(at, 2 * r + half) for at in (0, 1) for half in (0, 1)] for r in rows]
        mixed = mix_blocks([held] * 4, where, ro)
        for at, r in enumerate(rows):
            turned[pl.ds(r, 2 * BLOCKS, stride=stride), :] = mixed[
                :, at * 128 : at * 128 + 128
            ]
    lo = lo_ref[...]
    for half, ref in enumerate(o_refs):
        for first in range(0, BLOCKS, 14):
            x = jnp.concatenate(
                [
                    turned[
                        (half * BLOCKS + p) * stride : (half * BLOCKS + p) * stride + 64, :
                    ].astype(BF16)
                    for p in range(first, first + 14)
                ],
                axis=1,
            )
            ref[:, first * 128 : (first + 14) * 128] = matmul(lo, x).astype(BF16)


def both(own, other, matrix, ro, lo):
    hbm = pl.BlockSpec(memory_space=pltpu.HBM)
    return pl.pallas_call(
        functools.partial(both_kernel, matrix),
        in_specs=[WHOLE, WHOLE, hbm, hbm],
        out_specs=[WHOLE] * 2,
        out_shape=[jax.ShapeDtypeStruct((64, WIDTH), BF16)] * 2,
        scratch_shapes=[
            pltpu.VMEM((2, 128, BLOCKS, 128), BF16),
            pltpu.VMEM((2 * BLOCKS * 73, 128), F32),
            pltpu.SemaphoreType.DMA((2, 4)),
        ],
        compiler_params=pltpu.CompilerParams(vmem_limit_bytes=18 * MIB),
        cost_estimate=cost(10 * 64 * BLOCKS * WIDTH, 3),
        name=f"both{matrix}",
    )(ro, lo, own, other)


def block_scales(values, first, held):
    lanes = lax.broadcasted_iota(jnp.int32, held.shape, 1)
    for p in range(values.shape[1] // 128):
        block = jnp.abs(values[:, p * 128 : (p + 1) * 128].astype(F32))
        largest = jnp.max(block, axis=1, keepdims=True) / 1.5
        held = jnp.where(lanes == first + p, largest, held)
    return held


OUTPUTS = [
    jax.ShapeDtypeStruct((3, 2, 64, WIDTH), BF16),
    jax.ShapeDtypeStruct((3, 2, BLOCKS, 64), F32),
]


def last_kernel(lo_ref, x_ref, *refs):
    o_ref, s_ref, turned, held = refs[-4:]
    step = pl.program_id(0)
    tile = o_ref.shape[3]
    stride = 137

    @pl.when(step == 0)
    def _():
        for row in range(128):
            turned[pl.ds(row, BLOCKS, stride=stride), :] = x_ref[row].astype(F32)

    first = step * (tile // 128)
    x = jnp.concatenate(
        [
            turned[pl.ds((first + p) * stride, 128), :].astype(BF16)
            for p in range(tile // 128)
        ],
        axis=1,
    )
    values = matmul(lo_ref[...], x).astype(BF16)
    o_ref[...] = values.reshape(1, 2, 64, tile)
    scales = block_scales(values, first, held[...])
    held[...] = scales
    flat = scales.T
    s_ref[0, 0] = flat[:BLOCKS, :64]
    s_ref[0, 1] = flat[:BLOCKS, 64:]


def last(x, lo, matrix, rotated, scales):
    tile = 7168
    return pl.pallas_call(
        last_kernel,
        grid=(WIDTH // tile,),
        in_specs=[
            pl.BlockSpec((128, 128), lambda i: (0, 0)),
            pl.BlockSpec((128, BLOCKS, 128), lambda i: (0, 0, 0)),
            ORDER,
            ORDER,
        ],
        out_specs=[
            pl.BlockSpec((1, 2, 64, tile), lambda i: (matrix, 0, 0, i)),
            pl.BlockSpec((1, 2, BLOCKS, 64), lambda i: (matrix, 0, 0, 0)),
        ],
        out_shape=OUTPUTS,
        scratch_shapes=[
            pltpu.VMEM((BLOCKS * 137, 128), F32),
            pltpu.VMEM((128, 128), F32),
        ],
        input_output_aliases={2: 0, 3: 1},
        compiler_params=pltpu.CompilerParams(vmem_limit_bytes=24 * MIB),
        cost_estimate=cost(2 * 128 * 128 * WIDTH, 2),
        name=f"last{matrix}",
    )(lo, x, rotated, scales)


def place_kernel(half_ref, x_ref, *refs):
    o_ref, s_ref, held = refs[-3:]
    tile = o_ref.shape[3]
    values = x_ref[...]
    o_ref[...] = values.reshape(1, 1, 64, tile)
    scales = block_scales(values, pl.program_id(0) * (tile // 128), held[...])
    held[...] = scales
    s_ref[0, 0] = scales.T[:BLOCKS]


def place(x, half, matrix, into=()):
    tile = 7168
    return pl.pallas_call(
        place_kernel,
        grid_spec=pltpu.PrefetchScalarGridSpec(
            num_scalar_prefetch=1,
            grid=(WIDTH // tile,),
            in_specs=[pl.BlockSpec((64, tile), lambda i, half: (0, i))]
            + [ORDER] * len(into),
            out_specs=[
                pl.BlockSpec((1, 1, 64, tile), lambda i, half: (matrix, half[0], 0, i)),
                pl.BlockSpec((1, 1, BLOCKS, 64), lambda i, half: (matrix, half[0], 0, 0)),
            ],
            scratch_shapes=[pltpu.VMEM((64, 128), F32)],
        ),
        out_shape=OUTPUTS,
        input_output_aliases={2: 0, 3: 1} if into else {},
        compiler_params=pltpu.CompilerParams(vmem_limit_bytes=12 * MIB),
        cost_estimate=cost(64 * WIDTH, 1),
        name=f"place{matrix}",
    )(half, x, *into)


def gate(x, after):
    return pl.pallas_call(
        lambda *refs: None,
        in_specs=[ORDER] * (1 + len(after)),
        out_specs=ORDER,
        out_shape=jax.ShapeDtypeStruct(x.shape, x.dtype),
        input_output_aliases={0: 0},
        cost_estimate=pl.CostEstimate(flops=128, bytes_accessed=1024, transcendentals=0),
        name="gate",
    )(x, *after)


def swap(x, axis):
    return lax.ppermute(x, axis, [(0, 1), (1, 0)])


def local(weights, left_outer, left_inner, right_outer, right_inner):
    xh, xl, core = lax.axis_index(XH), lax.axis_index(XL), lax.axis_index(CORE)
    where = jnp.stack([xh, xl]).astype(jnp.int32)
    own_half = where[1:]

    lo = left_outer.reshape(64, 2, 32)
    lo = jnp.where(xh == 0, lo, lo[:, ::-1]).transpose(0, 2, 1)
    same = jnp.eye(2, dtype=BF16)
    same = jnp.where(xl == 0, same, same[::-1])
    lo2 = lo.reshape(1, 64, 32, 2, 1) * same.reshape(2, 1, 1, 1, 2)
    lo2 = lo2.reshape(128, 128)

    ro = right_outer.reshape(2, 2, BLOCKS, 2, 2, BLOCKS)
    ro = jnp.where(core == 0, ro[:, 0], ro[:, 1, :, :, ::-1])
    ro = ro.transpose(0, 1, 3, 2, 4)
    ro01 = jnp.where(xl == 0, ro, ro[::-1]).reshape(2 * BLOCKS, 4 * BLOCKS)
    ro2 = jnp.where(xl == 0, ro, ro[::-1, :, :, ::-1]).reshape(2 * BLOCKS, 4 * BLOCKS)

    sent01_shape = jax.ShapeDtypeStruct((128, 2, BLOCKS, 128), BF16)
    (sent01,) = inner(weights, (0, 1), None, left_inner, right_inner, [sent01_shape])
    came01 = lax.all_to_all(sent01, (XH, Y, Z, XL), 0, 0, tiled=True)

    keep2, send2 = inner(
        weights, (2,), where, left_inner, right_inner, [blocks_of(64)] * 2, [sent01]
    )
    came2 = swap(send2, XL)
    planes = right([keep2, came2, swap(keep2, CORE), swap(came2, CORE)], ro2)
    moved = {
        d: lax.ppermute(planes[d], (XH, XL), [(i, i ^ d) for i in range(4)])
        for d in (2, 1, 3)
    }
    sent2 = join([planes[0], moved[1], moved[2], moved[3]])
    came01 = gate(came01, [sent2])
    came2 = lax.all_to_all(sent2, (Y, Z), 0, 0, tiled=True)

    other01 = swap(came01, CORE)
    own0, send0 = both(came01, other01, 0, ro01, left_outer)
    own1, send1 = both(came01, other01, 1, ro01, left_outer)
    outputs = place(own0, own_half, 0)
    outputs = place(own1, own_half, 1, outputs)
    outputs = place(swap(send0, XL), 1 - own_half, 0, outputs)
    outputs = last(came2.reshape(128, BLOCKS, 128), lo2, 2, *outputs)
    rotated, scales = place(swap(send1, XL), 1 - own_half, 1, outputs)
    return rotated, scales.transpose(0, 1, 3, 2)


def solution(mesh):
    fine = Mesh(np.asarray(mesh.devices).reshape(SIZES), AXES)
    row, col = (XH, Y, Z), (XL, CORE)
    return jax.shard_map(
        local,
        mesh=fine,
        in_specs=(P(None, row, col), P(), P(), P(), P()),
        out_specs=(P(None, row, None, col), P(None, row, None, col)),
        check_vma=False,
    )
```

```python
import functools

import jax
import jax.numpy as jnp
import numpy as np
from jax import lax
from jax.experimental import pallas as pl
from jax.experimental.pallas import tpu as pltpu
from jax.sharding import Mesh
from jax.sharding import PartitionSpec as P

BF16 = jnp.bfloat16
F32 = jnp.float32
XH, Y, Z, XL, CORE = "xh", "y", "z", "xl", "core"
AXES = (XH, Y, Z, XL, CORE)
SIZES = (2, 4, 8, 2, 2)
WIDTH = 7168
BLOCKS = 56
MIB = 1024 * 1024
VMEM = 24 * MIB
INNER_VMEM = 60 * MIB
MICROS = 20
PITCH = BLOCKS + 1
WHOLE = pl.BlockSpec(memory_space=pltpu.VMEM)
ORDER = pl.BlockSpec(memory_space=pl.ANY)


def matmul(left, right):
    return jnp.dot(left, right, preferred_element_type=F32)


def blocks_of(count):
    return jax.ShapeDtypeStruct((count, BLOCKS, 128), BF16)


def cost(flops, passes):
    return pl.CostEstimate(
        flops=flops, bytes_accessed=passes * 128 * WIDTH * 2, transcendentals=0
    )


def inner_kernel(matrices, outs, *refs):
    if outs == 2:
        place_ref, refs = refs[0], refs[1:]
    w_ref, li_ref, ri_ref = refs[:3]
    o_refs, (held, turned, packed, sems, out_sems) = refs[-5 - outs : -5], refs[-5:]
    tiles = 1
    tile = WIDTH // tiles
    copies = [
        pltpu.make_async_copy(
            w_ref.at[matrix, :, pl.ds(t * tile, tile)],
            held.at[at * tiles + t],
            sems.at[at * tiles + t],
        )
        for at, matrix in enumerate(matrices)
        for t in range(tiles)
    ]
    for copy in copies:
        copy.start()
    ri = ri_ref[...]
    zero = jnp.zeros_like(ri)
    pair = jnp.concatenate(
        [
            jnp.concatenate([ri, zero], axis=1),
            jnp.concatenate([zero, ri], axis=1),
        ],
        axis=0,
    )
    li = li_ref[...]
    parts = []
    for place in range(len(matrices)):
        for t in range(tiles):
            which = place * tiles + t
            copies[which].wait()
            pairs = tile // 256
            stacked = jnp.concatenate(
                [held[which, :, c * 256 : (c + 1) * 256] for c in range(pairs)], axis=0
            )
            first = lax.dot_general(
                stacked, pair, (((1,), (1,)), ((), ())), preferred_element_type=F32
            ).astype(BF16)
            first = jnp.concatenate(
                [first[c * 128 : (c + 1) * 128] for c in range(pairs)], axis=1
            )
            second = matmul(li, first)
            for p in range(tile // 128):
                turned[pl.ds(t * (tile // 128) + p, 128, stride=PITCH), :] = second[
                    :, p * 128 : (p + 1) * 128
                ]
        for part in range(4):
            half = 1 - part // 2
            for r in range(32):
                if outs == 1:
                    to = part * 32 + r
                    row = to * PITCH
                else:
                    to = half * 64 + part % 2 * 32 + r
                    at = (place_ref[0] ^ (part % 2)) * 32 + r
                    row = (2 * at + (place_ref[1] ^ half)) * PITCH
                packed[place, to] = turned[pl.ds(row, BLOCKS), :].astype(BF16)
            if outs == 1:
                here, there = part * 32, o_refs[0].at[pl.ds(part * 32, 32), place]
            else:
                at = part % 2 * 32
                here, there = half * 64 + at, o_refs[half].at[pl.ds(at, 32)]
            parts.append(
                pltpu.make_async_copy(
                    packed.at[place, pl.ds(here, 32)], there, out_sems.at[len(parts)]
                )
            )
            parts[-1].start()
    for copy in parts:
        copy.wait()


def inner(weights, matrices, where, li, ri, shapes, after=()):
    hbm = pl.BlockSpec(memory_space=pltpu.HBM)
    count = len(matrices)
    scalars = [where] if len(shapes) == 2 else []
    return pl.pallas_call(
        functools.partial(inner_kernel, matrices, len(shapes)),
        in_specs=[pl.BlockSpec(memory_space=pltpu.SMEM)] * len(scalars)
        + [hbm, WHOLE, WHOLE]
        + [ORDER] * len(after),
        out_specs=[hbm] * len(shapes),
        out_shape=shapes,
        scratch_shapes=[
            pltpu.VMEM((1 * count, 128, WIDTH // 1), BF16),
            pltpu.VMEM((128 * PITCH, 128), F32),
            pltpu.VMEM((count, 128, BLOCKS, 128), BF16),
            pltpu.SemaphoreType.DMA((1 * count,)),
            pltpu.SemaphoreType.DMA((4 * count,)),
        ],
        compiler_params=pltpu.CompilerParams(vmem_limit_bytes=INNER_VMEM),
        cost_estimate=cost(4 * 128 * 128 * WIDTH, 2),
        name=f"inner{matrices[0]}",
    )(*scalars, weights, li, ri, *after)


def mix_blocks(refs, rows, ro):
    columns = jnp.concatenate(
        [
            jnp.concatenate([ref[at].astype(F32) for ref, at in zip(refs, where)], axis=0)
            for where in rows
        ],
        axis=1,
    )
    return matmul(ro, columns.astype(BF16))


def right_kernel(ro_ref, *refs):
    sources, (packed, sems) = refs[:4], refs[-2:]
    o_refs = refs[-6:-2]
    ro = ro_ref[...]
    copies = []
    for first in range(0, 64, 4):
        rows = range(first, first + 4)
        mixed = mix_blocks(sources, [(r,) * 4 for r in rows], ro)
        for at, r in enumerate(rows):
            lanes = slice(at * 128, at * 128 + 128)
            for half in range(2):
                block = mixed[half * BLOCKS : (half + 1) * BLOCKS, lanes]
                packed[r // 32 * 2 + half, r % 32] = block.astype(BF16)
        if first % 32 == 28:
            for to in (first // 32 * 2, first // 32 * 2 + 1):
                copies.append(pltpu.make_async_copy(packed.at[to], o_refs[to], sems.at[to]))
                copies[-1].start()
    for copy in copies:
        copy.wait()


def right(sources, ro, after=()):
    return pl.pallas_call(
        right_kernel,
        in_specs=[WHOLE] * 5 + [ORDER] * len(after),
        out_specs=[pl.BlockSpec(memory_space=pltpu.HBM)] * 4,
        out_shape=[blocks_of(32)] * 4,
        scratch_shapes=[
            pltpu.VMEM((4, 32, BLOCKS, 128), BF16),
            pltpu.SemaphoreType.DMA((4,)),
        ],
        compiler_params=pltpu.CompilerParams(vmem_limit_bytes=VMEM),
        cost_estimate=cost(1153 * 10**6 * MICROS, 3),
        name="right",
    )(ro, *sources, *after)


def join_kernel(*refs):
    o_ref, packed, sems = refs[-3:]
    copies = []
    for part in range(4):
        rows = pl.ds(part * 8, 8)
        for row in range(part * 8, part * 8 + 8):
            for at, ref in enumerate(refs[:4]):
                packed[row, at] = ref[row]
        copies.append(
            pltpu.make_async_copy(packed.at[rows], o_ref.at[rows], sems.at[part])
        )
        copies[-1].start()
    for copy in copies:
        copy.wait()


def join(pieces):
    return pl.pallas_call(
        join_kernel,
        in_specs=[WHOLE] * 4,
        out_specs=pl.BlockSpec(memory_space=pltpu.HBM),
        out_shape=jax.ShapeDtypeStruct((32, 4, BLOCKS, 128), BF16),
        scratch_shapes=[
            pltpu.VMEM((32, 4, BLOCKS, 128), BF16),
            pltpu.SemaphoreType.DMA((4,)),
        ],
        compiler_params=pltpu.CompilerParams(vmem_limit_bytes=VMEM),
        cost_estimate=cost(0, 2),
        name="join",
    )(*pieces)


def both_kernel(matrix, ro_ref, lo_ref, own_ref, other_ref, *refs):
    o_ref, held, turned, sems = refs[-4:]
    arriving = [
        [
            pltpu.make_async_copy(
                ref.at[pl.ds(part * 32, 32), matrix],
                held.at[at, pl.ds(part * 32, 32)],
                sems.at[at, part],
            )
            for at, ref in enumerate((own_ref, other_ref))
        ]
        for part in range(4)
    ]
    for part in arriving:
        for copy in part:
            copy.start()
    ro = ro_ref[...]
    stride = 73
    for first in range(0, 64, 4):
        if first % 16 == 0:
            for copy in arriving[first // 16]:
                copy.wait()
        rows = range(first, first + 4)
        where = [[(at, 2 * r + half) for at in (0, 1) for half in (0, 1)] for r in rows]
        mixed = mix_blocks([held] * 4, where, ro)
        for at, r in enumerate(rows):
            turned[pl.ds(r, BLOCKS, stride=stride), :] = mixed[
                :, at * 128 : at * 128 + 128
            ]
    lo = lo_ref[...]
    for first in range(0, BLOCKS, 14):
        x = jnp.concatenate(
            [
                turned[p * stride : p * stride + 64, :].astype(BF16)
                for p in range(first, first + 14)
            ],
            axis=1,
        )
        o_ref[:, first * 128 : (first + 14) * 128] = matmul(lo, x).astype(BF16)


def both(own, other, matrix, ro, lo, after=()):
    hbm = pl.BlockSpec(memory_space=pltpu.HBM)
    return pl.pallas_call(
        functools.partial(both_kernel, matrix),
        in_specs=[WHOLE, WHOLE, hbm, hbm] + [ORDER] * len(after),
        out_specs=WHOLE,
        out_shape=jax.ShapeDtypeStruct((64, WIDTH), BF16),
        scratch_shapes=[
            pltpu.VMEM((2, 128, BLOCKS, 128), BF16),
            pltpu.VMEM((BLOCKS * 73, 128), F32),
            pltpu.SemaphoreType.DMA((2, 4)),
        ],
        compiler_params=pltpu.CompilerParams(vmem_limit_bytes=18 * MIB),
        cost_estimate=cost(10 * 64 * BLOCKS * WIDTH, 3),
        name=f"both{matrix}",
    )(ro, lo, own, other, *after)


def block_scales(values, first, held):
    lanes = lax.broadcasted_iota(jnp.int32, held.shape, 1)
    for p in range(values.shape[1] // 128):
        block = jnp.abs(values[:, p * 128 : (p + 1) * 128].astype(F32))
        largest = jnp.max(block, axis=1, keepdims=True) / 1.5
        held = jnp.where(lanes == first + p, largest, held)
    return held


OUTPUTS = [
    jax.ShapeDtypeStruct((3, 2, 64, WIDTH), BF16),
    jax.ShapeDtypeStruct((3, 2, BLOCKS, 64), F32),
]


def last_kernel(lo_ref, x_ref, *refs):
    o_ref, s_ref, turned, held = refs[-4:]
    step = pl.program_id(0)
    tile = o_ref.shape[3]
    stride = 137

    @pl.when(step == 0)
    def _():
        for row in range(128):
            turned[pl.ds(row, BLOCKS, stride=stride), :] = x_ref[row].astype(F32)

    first = step * (tile // 128)
    x = jnp.concatenate(
        [
            turned[pl.ds((first + p) * stride, 128), :].astype(BF16)
            for p in range(tile // 128)
        ],
        axis=1,
    )
    values = matmul(lo_ref[...], x).astype(BF16)
    o_ref[...] = values.reshape(1, 2, 64, tile)
    scales = block_scales(values, first, held[...])
    held[...] = scales
    flat = scales.T
    s_ref[0, 0] = flat[:BLOCKS, :64]
    s_ref[0, 1] = flat[:BLOCKS, 64:]


def last(x, lo, matrix, rotated, scales):
    tile = 7168
    return pl.pallas_call(
        last_kernel,
        grid=(WIDTH // tile,),
        in_specs=[
            pl.BlockSpec((128, 128), lambda i: (0, 0)),
            pl.BlockSpec((128, BLOCKS, 128), lambda i: (0, 0, 0)),
            ORDER,
            ORDER,
        ],
        out_specs=[
            pl.BlockSpec((1, 2, 64, tile), lambda i: (matrix, 0, 0, i)),
            pl.BlockSpec((1, 2, BLOCKS, 64), lambda i: (matrix, 0, 0, 0)),
        ],
        out_shape=OUTPUTS,
        scratch_shapes=[
            pltpu.VMEM((BLOCKS * 137, 128), F32),
            pltpu.VMEM((128, 128), F32),
        ],
        input_output_aliases={2: 0, 3: 1},
        compiler_params=pltpu.CompilerParams(vmem_limit_bytes=24 * MIB),
        cost_estimate=cost(2 * 128 * 128 * WIDTH, 2),
        name=f"last{matrix}",
    )(lo, x, rotated, scales)


def place_kernel(half_ref, x_ref, *refs):
    o_ref, s_ref, held = refs[-3:]
    tile = o_ref.shape[3]
    values = x_ref[...]
    o_ref[...] = values.reshape(1, 1, 64, tile)
    scales = block_scales(values, pl.program_id(0) * (tile // 128), held[...])
    held[...] = scales
    s_ref[0, 0] = scales.T[:BLOCKS]


def place(x, half, matrix, into=()):
    tile = 7168
    return pl.pallas_call(
        place_kernel,
        grid_spec=pltpu.PrefetchScalarGridSpec(
            num_scalar_prefetch=1,
            grid=(WIDTH // tile,),
            in_specs=[pl.BlockSpec((64, tile), lambda i, half: (0, i))]
            + [ORDER] * len(into),
            out_specs=[
                pl.BlockSpec((1, 1, 64, tile), lambda i, half: (matrix, half[0], 0, i)),
                pl.BlockSpec((1, 1, BLOCKS, 64), lambda i, half: (matrix, half[0], 0, 0)),
            ],
            scratch_shapes=[pltpu.VMEM((64, 128), F32)],
        ),
        out_shape=OUTPUTS,
        input_output_aliases={2: 0, 3: 1} if into else {},
        compiler_params=pltpu.CompilerParams(vmem_limit_bytes=12 * MIB),
        cost_estimate=cost(64 * WIDTH, 1),
        name=f"place{matrix}",
    )(half, x, *into)


def gate(x, after):
    return pl.pallas_call(
        lambda *refs: None,
        in_specs=[ORDER] * (1 + len(after)),
        out_specs=ORDER,
        out_shape=jax.ShapeDtypeStruct(x.shape, x.dtype),
        input_output_aliases={0: 0},
        cost_estimate=pl.CostEstimate(flops=128, bytes_accessed=1024, transcendentals=0),
        name="gate",
    )(x, *after)


def swap(x, axis):
    return lax.ppermute(x, axis, [(0, 1), (1, 0)])


def local(weights, left_outer, left_inner, right_outer, right_inner):
    xh, xl, core = lax.axis_index(XH), lax.axis_index(XL), lax.axis_index(CORE)
    where = jnp.stack([xh, xl]).astype(jnp.int32)
    own_half = where[1:]

    lo = left_outer.reshape(64, 2, 32)
    lo = jnp.where(xh == 0, lo, lo[:, ::-1]).transpose(0, 2, 1)
    same = jnp.eye(2, dtype=BF16)
    same = jnp.where(xl == 0, same, same[::-1])
    lo2 = lo.reshape(1, 64, 32, 2, 1) * same.reshape(2, 1, 1, 1, 2)
    lo2 = lo2.reshape(128, 128)

    ro = right_outer.reshape(2, 2, BLOCKS, 2, 2, BLOCKS)
    ro = jnp.where(core == 0, ro[:, 0], ro[:, 1, :, :, ::-1])
    ro = ro.transpose(0, 1, 3, 2, 4)
    ro01 = jnp.where(xl == 0, ro, ro[::-1]).reshape(2 * BLOCKS, 4 * BLOCKS)
    ro2 = jnp.where(xl == 0, ro, ro[::-1, :, :, ::-1]).reshape(2 * BLOCKS, 4 * BLOCKS)

    sent01_shape = jax.ShapeDtypeStruct((128, 2, BLOCKS, 128), BF16)
    (sent01,) = inner(weights, (0, 1), None, left_inner, right_inner, [sent01_shape])
    came01 = lax.all_to_all(sent01, (XH, Y, Z, XL), 0, 0, tiled=True)

    keep2, send2 = inner(
        weights, (2,), where, left_inner, right_inner, [blocks_of(64)] * 2, [sent01]
    )
    came2 = swap(send2, XL)
    planes = right([keep2, came2, swap(keep2, CORE), swap(came2, CORE)], ro2)
    moved = {
        d: lax.ppermute(planes[d], (XH, XL), [(i, i ^ d) for i in range(4)])
        for d in (2, 1, 3)
    }
    sent2 = join([planes[0], moved[1], moved[2], moved[3]])
    came01 = gate(came01, [sent2])
    came2 = lax.all_to_all(sent2, (Y, Z), 0, 0, tiled=True)

    other01 = swap(came01, CORE)
    ro_own, ro_partner = ro01[:BLOCKS], ro01[BLOCKS:]
    send0 = both(came01, other01, 0, ro_partner, left_outer)
    send1 = both(came01, other01, 1, ro_partner, left_outer, [send0])
    own0 = both(came01, other01, 0, ro_own, left_outer, [send1])
    own1 = both(came01, other01, 1, ro_own, left_outer, [own0])
    outputs = place(own0, own_half, 0)
    outputs = place(own1, own_half, 1, outputs)
    outputs = place(swap(send0, XL), 1 - own_half, 0, outputs)
    outputs = place(swap(send1, XL), 1 - own_half, 1, outputs)
    rotated, scales = last(came2.reshape(128, BLOCKS, 128), lo2, 2, *outputs)
    return rotated, scales.transpose(0, 1, 3, 2)


def solution(mesh):
    fine = Mesh(np.asarray(mesh.devices).reshape(SIZES), AXES)
    row, col = (XH, Y, Z), (XL, CORE)
    return jax.shard_map(
        local,
        mesh=fine,
        in_specs=(P(None, row, col), P(), P(), P(), P()),
        out_specs=(P(None, row, None, col), P(None, row, None, col)),
        check_vma=False,
    )
```
